256 devices in a mesh: ctx: 64 (over x, z, core), head: 4 (over y).
Axes of the slice: x: 4, y: 4, z: 8, core: 2. Of those that a mesh axis runs over, the one named last changes fastest.
Arguments:
- q_lin: bfloat16 [32768, 8192], P('ctx', 'head'), may hold values from -6 to 6
- k_lin: bfloat16 [32768, 8192], P('ctx', 'head'), may hold values from -6 to 6
- v_lin: bfloat16 [32768, 8192], P('ctx', 'head'), may hold values from -24 to 24
- lin_gain: float32 [8192], P('head'), may hold values from 0.1 to 1.9
- q_soft: bfloat16 [32768, 8192], P('ctx', 'head'), may hold values from -64 to 64
- k_soft: bfloat16 [32768, 1024], P('ctx', 'head'), may hold values from -6 to 6
- v_soft: bfloat16 [32768, 1024], P('ctx', 'head'), may hold values from -6 to 6
- doc_lengths: int32 [32], replicated, may hold values from 1 to 2048, 32768 in all
Outputs:
- lin_out: bfloat16 [32768, 8192], P('ctx', 'head')
- attn_out: bfloat16 [32768, 8192], P('ctx', 'head')
The draws below stay inside these ranges and needn't reach their ends.
Inputs may be any that keep to these rules, and one draw needn't show every extreme that they name: `doc_lengths`: document lengths sum to 32768; the longest is exactly 2048.
All inputs are finite; a program needn't handle non-finite values.
Results may differ from the reference program's by a relative error of at most 0.013.
Values may be sent and summed in bfloat16 or wider, within the bound.
No kernel may reach another device: no remote copies, remote signals or barrier semaphores. Data moves between devices by JAX's collectives and lax.ppermute only.
A program may use at most 256 MiB of HBM per device.

```python
import math
import jax
import jax.numpy as jnp
import numpy as np
from jax import lax

H = 64
HD = 128
KV = 8
TOK_DEV = 512
REACH = 4
TOKENS = 32768
DOC_MOST = 2048
DOCS = 32
N_CTX = 64


def shared_keys(key):
    return jax.random.normal(key, (TOKENS, KV, HD), jnp.float32)


def draw_k_soft(key, part):
    base_keys = shared_keys(key)
    return jnp.clip(base_keys, -6.0, 6.0).reshape(TOKENS, KV * HD).astype(jnp.bfloat16)


def draw_q_soft(key, part):
    key = jax.random.fold_in(key, 5)
    queries = jax.random.normal(key, (TOKENS, H, HD), jnp.float32)
    return jnp.clip(queries, -64.0, 64.0).reshape(TOKENS, H * HD).astype(jnp.bfloat16)


def draw_v_lin(key, part):
    key = jax.random.fold_in(key, 7)
    feature_ramp = 0.5 * 3.0 ** (jnp.arange(H * HD, dtype=jnp.float32) / (H * HD))
    factor = jnp.exp(jax.random.uniform(jax.random.fold_in(key, 1), (H * HD,), jnp.float32, jnp.log(0.5), jnp.log(2.0)))
    normal_part = jax.random.normal(key, (TOKENS, H * HD), jnp.float32)
    values = normal_part * feature_ramp[None, :] * factor[None, :]
    return jnp.clip(values, -24.0, 24.0).astype(jnp.bfloat16)


def steps_of(stream_key, dims, cuts, low, top_value):
    gain = 1.0
    for position, parts in cuts:
        heights = jax.random.uniform(jax.random.fold_in(jax.random.fold_in(stream_key, 6), position), (parts,), jnp.float32, low / len(cuts), top_value / len(cuts))
        gain = gain * jnp.repeat(jnp.exp(heights), dims[position] // parts).reshape((-1,) + (1,) * (len(dims) - 1 - position))
    return gain


def length_profile(count, total, bound, slope):
    portions = [(1 << 20) // math.isqrt(standing ** slope) + 1 for standing in range(2, count + 1)]
    surplus, given = total - bound - (count - 1), [1] * (count - 1)
    while surplus > 0:
        movable = [i for i in range(count - 1) if given[i] < bound]
        pool, left = sum([portions[i] for i in movable]), surplus
        for i in movable:
            more = min(bound - given[i], max(1, left * portions[i] // pool), surplus)
            given[i] = given[i] + more
            surplus = surplus - more
    return np.array([bound] + given)


def uneven(own_key, count, total, most, lean):
    if count == 2:
        one = jax.random.randint(own_key, (), max(1, total - most), min(most, total - 1) + 1)
        return jnp.stack([one, total - one])
    tallies = jnp.asarray(length_profile(count, total, most, lean), jnp.int32)
    twos = (count - 1) // 2
    donor, receiver = tallies[1:1 + 2 * twos:2], tallies[2:2 + 2 * twos:2]
    margin = jnp.minimum(donor - 1, most - receiver)
    moved = jax.random.randint(jax.random.fold_in(own_key, 1), (twos,), 0, 1 << 20) % (margin + 1)
    tallies = tallies.at[1:1 + 2 * twos:2].set(donor - moved).at[2:2 + 2 * twos:2].set(receiver + moved)
    return tallies[jax.random.permutation(jax.random.fold_in(own_key, 2), count)]


def centred(own_key, dims, deviation, most, cuts=(), kind=jnp.bfloat16):
    array = jax.random.normal(own_key, dims, jnp.float32) * deviation
    if len(cuts) > 0:
        array = steps_of(own_key, dims, cuts, -0.22, 0.18) * array
    return jnp.clip(array, min=-most, max=most).astype(kind)


def setup_inputs(seed: int = 0) -> dict:
    seeds = jax.random.split(jax.random.key(seed), 9)
    return {
        "q_lin": centred(seeds[0], (TOKENS, H * HD), 1.0, 6.0, ((0, 64), (1, 4))),
        "k_lin": centred(seeds[1], (TOKENS, H * HD), 1.0, 6.0, ((0, 64), (1, 4))),
        "v_lin": draw_v_lin(jax.random.fold_in(seeds[8], 71), 0),
        "lin_gain": jnp.clip(1.0 + 0.18 * jax.random.normal(seeds[3], (H * HD,), jnp.float32), 0.1, 1.9),
        "q_soft": draw_q_soft(jax.random.fold_in(seeds[8], 71), 0),
        "k_soft": draw_k_soft(jax.random.fold_in(seeds[8], 71), 0),
        "v_soft": centred(seeds[6], (TOKENS, KV * HD), 1.0, 6.0, ((0, 64), (1, 4))),
        "doc_lengths": uneven(seeds[7], DOCS, TOKENS, DOC_MOST, 2).astype(jnp.int32),
    }


epsilon = 1e-05

def document_ids(doc_lengths):
    doc_starts = jnp.cumsum(doc_lengths) - doc_lengths
    positions = jnp.arange(-1, TOKENS, dtype=jnp.int32)
    return lax.optimization_barrier(jnp.sum((doc_starts[None, :] <= positions[:, None]).astype(jnp.int32), axis=1)) - 1

def linear_part(q_lin, k_lin, v_lin, lin_gain, ids_all):
    doc_ids = ids_all[1:].reshape(N_CTX, TOK_DEV)
    prev_ids = ids_all[:-1].reshape(N_CTX, TOK_DEV)[:, 0]
    q_heads = q_lin.reshape(N_CTX, TOK_DEV, H, HD)
    k_heads = k_lin.reshape(N_CTX, TOK_DEV, H, HD)
    v_heads = v_lin.reshape(N_CTX, TOK_DEV, H, HD)
    lower_mask = jnp.tril(jnp.ones((TOK_DEV, TOK_DEV), dtype=bool))

    def step(run_state, block_data):
        q_block, k_block, v_block, block_ids, prev_id = block_data
        same_doc = (block_ids[:, None] == block_ids[None, :]) & lower_mask
        scores = jnp.einsum('thd,shd->hts', q_block.astype(jnp.float32), k_block.astype(jnp.float32))
        scores = lax.optimization_barrier(jnp.where(same_doc[None], scores, 0.0).astype(jnp.bfloat16))
        inside = jnp.einsum('hts,shd->thd', scores.astype(jnp.float32), v_block.astype(jnp.float32))
        state_round = lax.optimization_barrier(run_state.astype(jnp.bfloat16))
        carried_term = jnp.einsum('thd,hde->the', q_block.astype(jnp.float32), state_round.astype(jnp.float32))
        carried = (block_ids == block_ids[0]) & (block_ids[0] == prev_id)
        mixture = inside + jnp.where(carried[:, None, None], carried_term, 0.0)
        squares = lax.optimization_barrier(jnp.mean(mixture * mixture, axis=(1, 2)))
        normed = (mixture.reshape(TOK_DEV, H * HD) * lax.rsqrt(squares + epsilon)[:, None] * lin_gain[None, :]).astype(jnp.bfloat16)
        in_tail = block_ids == block_ids[-1]
        local_state = jnp.einsum('thd,the->hde', jnp.where(in_tail[:, None, None], k_block.astype(jnp.float32), 0.0), v_block.astype(jnp.float32))
        reset_flag = (block_ids[0] != prev_id) | (block_ids[0] != block_ids[-1])
        next_state = local_state + jnp.where(reset_flag, 0.0, run_state)
        return (next_state, normed)
    zero_state = jnp.zeros((H, HD, HD), jnp.float32)
    _, block_outs = lax.scan(step, zero_state, (q_heads, k_heads, v_heads, doc_ids, prev_ids))
    return block_outs.reshape(TOKENS, H * HD)

def softmax_part(q_soft, k_soft, v_soft, ids_all):
    group_size = H // KV
    pad_rows = REACH * TOK_DEV
    key_span = (REACH + 1) * TOK_DEV
    doc_ids = ids_all[1:]
    k_padded = jnp.concatenate([jnp.zeros((pad_rows, KV * HD), jnp.bfloat16), k_soft], 0)
    v_padded = jnp.concatenate([jnp.zeros((pad_rows, KV * HD), jnp.bfloat16), v_soft], 0)
    id_padded = jnp.concatenate([jnp.full((pad_rows,), -1, jnp.int32), doc_ids])
    score_scale = 1.0 / math.sqrt(HD)

    def block(block_index):
        block_begin = (block_index * TOK_DEV).astype(jnp.int32)
        q_block = lax.dynamic_slice_in_dim(q_soft, block_begin, TOK_DEV, 0).reshape(TOK_DEV, KV, group_size, HD)
        k_block = lax.dynamic_slice_in_dim(k_padded, block_begin, key_span, 0).reshape(key_span, KV, HD)
        v_block = lax.dynamic_slice_in_dim(v_padded, block_begin, key_span, 0).reshape(key_span, KV, HD)
        query_ids = lax.dynamic_slice_in_dim(doc_ids, block_begin, TOK_DEV, 0)
        key_ids = lax.dynamic_slice_in_dim(id_padded, block_begin, key_span, 0)
        query_pos = block_begin + jnp.arange(TOK_DEV, dtype=jnp.int32)
        key_pos = block_begin - pad_rows + jnp.arange(key_span, dtype=jnp.int32)
        visible = (query_ids[:, None] == key_ids[None, :]) & (key_pos[None, :] <= query_pos[:, None])
        logits = jnp.einsum('tkgd,skd->kgts', q_block.astype(jnp.float32), k_block.astype(jnp.float32)) * score_scale
        logits = jnp.where(visible, logits, -1e+30)
        row_top = lax.optimization_barrier(jnp.max(logits, axis=-1, keepdims=True))
        weights = jnp.where(visible, jnp.exp(logits - row_top), 0.0)
        row_total = lax.optimization_barrier(jnp.sum(weights, axis=-1))
        weights_round = lax.optimization_barrier(weights.astype(jnp.bfloat16))
        running = jnp.einsum('kgts,skd->kgtd', weights_round.astype(jnp.float32), v_block.astype(jnp.float32))
        result = running / row_total[..., None]
        return result.transpose(2, 0, 1, 3).reshape(TOK_DEV, H * HD).astype(jnp.bfloat16)
    block_outs = lax.map(block, jnp.arange(N_CTX, dtype=jnp.int32))
    return block_outs.reshape(TOKENS, H * HD)

def reference(q_lin, k_lin, v_lin, lin_gain, q_soft, k_soft, v_soft, doc_lengths):
    ids_all = document_ids(doc_lengths)
    lin_out = linear_part(q_lin, k_lin, v_lin, lin_gain, ids_all)
    attn_out = softmax_part(q_soft, k_soft, v_soft, ids_all)
    return (lin_out, attn_out)
```

```python
import functools
import math

import jax
import jax.numpy as jnp
from jax import lax
from jax.experimental import pallas as pl
from jax.experimental.pallas import tpu as pltpu
from jax.sharding import PartitionSpec as P

H = 64
HD = 128
EPS = 1e-05
BIG = 1e30
LOW = 2.0**-60
HIGH = 2.0**100
C2 = math.log2(math.e) / math.sqrt(HD)
BF = jnp.bfloat16
F32 = jnp.float32
VMEM_LIMIT = 32 * 1024 * 1024


def doc_start(meta, pos):
    total, start = jnp.int32(0), jnp.int32(0)
    for d in range(1, meta.shape[0]):
        start = jnp.where(total <= pos, total, start)
        total = total + meta[d]
    return start


def doc_end(meta, pos):
    total, end = jnp.int32(0), jnp.int32(0)
    for d in range(1, meta.shape[0]):
        end = jnp.where(total <= pos, total + meta[d], end)
        total = total + meta[d]
    return end


def doc_rows(meta):
    lane = lax.broadcasted_iota(jnp.int32, (1, HD), 1)
    start = jnp.full((1, HD), 1 << 30, jnp.int32)
    end = jnp.full((1, HD), 1 << 30, jnp.int32)
    total = jnp.int32(0)
    for d in range(1, meta.shape[0]):
        start = jnp.where(lane == d - 1, total, start)
        total = total + meta[d]
        end = jnp.where(lane == d - 1, total, end)
    return start, end


def member(meta, first, count):
    start, end = doc_rows(meta)
    pos = first + lax.broadcasted_iota(jnp.int32, (count, HD), 0)
    return (pos >= start) & (pos < end)


def params(limit=VMEM_LIMIT):
    return pltpu.CompilerParams(vmem_limit_bytes=limit)


def qk(q, k):
    return lax.dot_general(q, k, (((1,), (1,)), ((), ())), preferred_element_type=F32)


def state_kernel(meta, k_ref, v_ref, keep_ref, send_ref):
    i = pl.program_id(0)
    rows = k_ref.shape[0]
    per = k_ref.shape[1] // HD
    b = meta[0]
    tail = doc_start(meta, b * rows + rows - 1) - b * rows
    row = lax.broadcasted_iota(jnp.int32, (rows, 2 * HD), 0)
    live = row >= tail

    def write(out_ref, base):
        for j in range(0, per, 2):
            cols = slice(j * HD, (j + 2) * HD)
            k = jnp.where(live, k_ref[:, cols], jnp.zeros((rows, 2 * HD), BF))
            s = lax.dot_general(
                k, v_ref[:, cols], (((0,), (0,)), ((), ())), preferred_element_type=F32
            ).astype(BF)
            for e in range(2):
                part = slice(e * HD, (e + 1) * HD)
                out_ref[pl.ds(pl.multiple_of(base + (j + e) * HD, HD), HD), :] = s[part, part]

    half = pl.num_programs(0) // 2

    @pl.when(i < half)
    def _():
        write(keep_ref, i * per * HD)

    @pl.when(i >= half)
    def _():
        write(send_ref, (i - half) * per * HD)


def local_state(meta, k_lin, v_lin, steps=4):
    rows, cols = k_lin.shape
    block = cols // steps
    spec = pl.BlockSpec((rows, block), lambda i, m: (0, (i + (steps // 2) * (m[0] % 2)) % steps))
    half = (cols // 2, HD)
    return pl.pallas_call(
        state_kernel,
        grid_spec=pltpu.PrefetchScalarGridSpec(
            num_scalar_prefetch=1,
            grid=(steps,),
            in_specs=[spec, spec],
            out_specs=[pl.BlockSpec(half, lambda i, m: (0, 0))] * 2,
        ),
        out_shape=[jax.ShapeDtypeStruct(half, BF)] * 2,
        compiler_params=params(62 * 1024 * 1024),
        name="local_state",
    )(meta, k_lin, v_lin)


def chip_kernel(rows, meta, own_ref, got_ref, out_ref):
    b = meta[0]
    second = b - b % 2 + 1
    whole = (doc_start(meta, second * rows + rows - 1) < second * rows).astype(F32)
    odd = (b % 2).astype(F32)
    scale_own = odd + (1.0 - odd) * whole
    scale_got = (1.0 - odd) + odd * whole
    out_ref[...] = (scale_own * own_ref[...].astype(F32) + scale_got * got_ref[...].astype(F32)).astype(BF)


def chip_state(meta, own, got, rows):
    return pl.pallas_call(
        functools.partial(chip_kernel, rows),
        in_specs=[pl.BlockSpec(memory_space=pltpu.SMEM)] + [pl.BlockSpec(memory_space=pltpu.VMEM)] * 2,
        out_specs=pl.BlockSpec(memory_space=pltpu.VMEM),
        out_shape=jax.ShapeDtypeStruct(own.shape, BF),
        compiler_params=params(),
        name="chip_state",
    )(meta, own, got)


def enter_kernel(rows, meta, one_ref, two_ref, own_ref, got_ref, mine_ref, pay_ref):
    b = meta[0]
    first = b - b % 2
    before = first * rows - 2 * rows
    chained = (doc_start(meta, first * rows - 1) < before).astype(F32)
    passes = (doc_start(meta, first * rows + rows - 1) < first * rows).astype(F32)
    odd = (b % 2).astype(F32)
    even = 1.0 - odd
    state = one_ref[...].astype(F32) + chained * two_ref[...].astype(F32)
    mine_ref[...] = ((even + odd * passes) * state + odd * got_ref[...].astype(F32)).astype(BF)
    pay_ref[...] = ((odd + even * passes) * state + even * own_ref[...].astype(F32)).astype(BF)


def entering(meta, one, two, own, got, rows):
    return pl.pallas_call(
        functools.partial(enter_kernel, rows),
        in_specs=[pl.BlockSpec(memory_space=pltpu.SMEM)] + [pl.BlockSpec(memory_space=pltpu.VMEM)] * 4,
        out_specs=[pl.BlockSpec(memory_space=pltpu.VMEM)] * 2,
        out_shape=[jax.ShapeDtypeStruct(own.shape, BF)] * 2,
        compiler_params=params(),
        name="entering",
    )(meta, one, two, own, got)


def inside_kernel(meta, q_ref, k_ref, v_ref, out_ref, mask_ref):
    rows = q_ref.shape[0]
    half = rows // 2
    b = meta[0]

    @pl.when(pl.program_id(0) == 0)
    def _():
        start, _ = doc_rows(meta)
        pos = b * rows + lax.broadcasted_iota(jnp.int32, (rows, HD), 0)
        began = jnp.max(jnp.where(pos >= start, start, -1), axis=1, keepdims=True) - b * rows
        row = lax.broadcasted_iota(jnp.int32, (rows, rows), 0)
        col = lax.broadcasted_iota(jnp.int32, (rows, rows), 1)
        mask_ref[...] = jnp.where((col <= row) & (col >= began), 1.0, 0.0).astype(BF)

    for j in range(q_ref.shape[1] // HD):
        cols = slice(j * HD, (j + 1) * HD)
        pair = slice((j - j % 2) * HD, (j - j % 2 + 2) * HD)
        part = slice((j % 2) * HD, (j % 2 + 1) * HD)
        for i in range(2):
            at, upto = slice(i * half, (i + 1) * half), slice(0, (i + 1) * half)
            s = qk(q_ref[at, cols], k_ref[upto, cols]).astype(BF) * mask_ref[at, upto]
            o = jnp.dot(s, v_ref[upto, pair], preferred_element_type=F32)
            out_ref[at, cols] = o[:, part].astype(BF)


def inside_part(meta, q_lin, k_lin, v_lin, steps=4):
    rows, cols = q_lin.shape
    spec = pl.BlockSpec((rows, cols // steps), lambda i, m: (0, i))
    return pl.pallas_call(
        inside_kernel,
        grid_spec=pltpu.PrefetchScalarGridSpec(
            num_scalar_prefetch=1,
            grid=(steps,),
            in_specs=[spec] * 3,
            out_specs=spec,
            scratch_shapes=[pltpu.VMEM((rows, rows), BF)],
        ),
        out_shape=jax.ShapeDtypeStruct((rows, cols), BF),
        compiler_params=params(61 * 1024 * 1024),
        name="inside",
    )(meta, q_lin, k_lin, v_lin)


def carried_kernel(meta, q_ref, in_ref, mine_ref, other_ref, mix_ref, sum_ref, acc_ref):
    i = pl.program_id(0)
    half = pl.num_programs(0) // 2
    rows = q_ref.shape[0]
    per = q_ref.shape[1] // HD
    b = meta[0]
    first = b * rows
    reach = jnp.where(doc_start(meta, first) < first, doc_end(meta, first) - first, 0)
    row = lax.broadcasted_iota(jnp.int32, (rows, 2 * HD), 0)
    live = row < reach
    none = jnp.zeros((HD, HD), BF)

    @pl.when(i == 0)
    def _():
        acc_ref[...] = jnp.zeros_like(acc_ref)

    def work(state_ref, base):
        squares = acc_ref[...]
        for j in range(0, per, 2):
            cols = slice(j * HD, (j + 2) * HD)
            one, two = (
                state_ref[pl.ds(pl.multiple_of(base + (j + e) * HD, HD), HD), :] for e in range(2)
            )
            state = jnp.concatenate(
                [jnp.concatenate([one, none], axis=1), jnp.concatenate([none, two], axis=1)], axis=0
            )
            term = jnp.dot(q_ref[:, cols], state, preferred_element_type=F32)
            mix = in_ref[:, cols].astype(F32) + jnp.where(live, term, 0.0)
            square = mix * mix
            squares = squares + (square[:, :HD] + square[:, HD:])
            mix_ref[:, cols] = mix.astype(BF)
        acc_ref[...] = squares

    @pl.when(i < half)
    def _():
        work(mine_ref, i * per * HD)

    @pl.when(i >= half)
    def _():
        work(other_ref, (i - half) * per * HD)

    @pl.when(i == pl.num_programs(0) - 1)
    def _():
        sum_ref[...] = jnp.sum(acc_ref[...].T, axis=0, keepdims=True)


def carried_part(meta, q_lin, inside, mine, other, steps=4):
    rows, cols = q_lin.shape
    spec = pl.BlockSpec(
        (rows, cols // steps), lambda i, m: (0, (i + (steps // 2) * (m[0] % 2)) % steps)
    )
    whole = pl.BlockSpec(mine.shape, lambda i, m: (0, 0))
    return pl.pallas_call(
        carried_kernel,
        grid_spec=pltpu.PrefetchScalarGridSpec(
            num_scalar_prefetch=1,
            grid=(steps,),
            in_specs=[spec, spec, whole, whole],
            out_specs=[spec, pl.BlockSpec((1, rows), lambda i, m: (0, 0))],
            scratch_shapes=[pltpu.VMEM((rows, HD), F32)],
        ),
        out_shape=[jax.ShapeDtypeStruct((rows, cols), BF), jax.ShapeDtypeStruct((1, rows), F32)],
        compiler_params=params(),
        name="carried",
    )(meta, q_lin, inside, mine, other)


def norm_kernel(mix_ref, a_ref, b_ref, gain_ref, out_ref):
    rows = mix_ref.shape[0]
    total = a_ref[...] + b_ref[...]
    inv = lax.rsqrt(total / (H * HD) + EPS)
    inv = jnp.broadcast_to(inv, (HD, rows)).T
    for j in range(mix_ref.shape[1] // HD):
        cols = slice(j * HD, (j + 1) * HD)
        out_ref[:, cols] = (mix_ref[:, cols].astype(F32) * inv * gain_ref[:, cols]).astype(BF)


def norm_part(mix, sums, gain, steps=4):
    rows, cols = mix.shape
    spec = pl.BlockSpec((rows, cols // steps), lambda i: (0, i))
    one = pl.BlockSpec((1, rows), lambda i: (0, 0))
    return pl.pallas_call(
        norm_kernel,
        grid=(steps,),
        in_specs=[spec, one, one, pl.BlockSpec((1, cols // steps), lambda i: (0, i))],
        out_specs=spec,
        out_shape=jax.ShapeDtypeStruct((rows, cols), BF),
        compiler_params=params(),
        name="norm",
    )(mix, *sums, gain)


def fill(meta, k_buf, v_buf, slot, k_ref, v_ref, first, count):
    at = slice(slot * count, (slot + 1) * count)
    k_buf[at, :HD] = k_ref[...]
    k_buf[at, HD:] = jnp.where(member(meta, first, count), 0.0, -BIG).astype(BF)
    v_buf[at, :HD] = v_ref[...]
    v_buf[at, HD:] = jnp.ones((count, HD), BF)


def mask_queries(meta, qx_ref, first, count):
    qx_ref[...] = jnp.where(member(meta, first, count), 1.0, 0.0).astype(BF)


def join_kernel(k_ref, v_ref, out_ref):
    width = k_ref.shape[1]
    out_ref[:, :width] = k_ref[...]
    out_ref[:, width:] = v_ref[...]


def joined(k, v):
    rows, width = k.shape
    return pl.pallas_call(
        join_kernel,
        in_specs=[pl.BlockSpec(memory_space=pltpu.VMEM)] * 2,
        out_specs=pl.BlockSpec(memory_space=pltpu.VMEM),
        out_shape=jax.ShapeDtypeStruct((rows, 2 * width), k.dtype),
        compiler_params=params(62 * 1024 * 1024),
        name="join",
    )(k, v)


def attend(q_ref, qx_ref, k_buf, v_buf, acc_ref, total_ref, keys, causal=None, add=True):
    lane = lax.broadcasted_iota(jnp.int32, total_ref.shape, 1)
    packed = total_ref[...] if add else jnp.zeros(total_ref.shape, F32)
    for h in range(q_ref.shape[1] // HD):
        cols = slice(h * HD, (h + 1) * HD)
        q = jnp.concatenate([q_ref[:, cols], qx_ref[...]], axis=1)
        p = jnp.exp2(qk(q, k_buf[keys, :]) * C2)
        if causal is not None:
            p = jnp.where(causal, p, 0.0)
        o = jnp.dot(p.astype(BF), v_buf[keys, :], preferred_element_type=F32)
        if add:
            acc_ref[:, cols] += o[:, :HD]
        else:
            acc_ref[:, cols] = o[:, :HD]
        packed = packed + jnp.where(lane == h, o[:, HD:], 0.0)
    total_ref[...] = packed


def add_earlier(meta, rows, work, slots):
    half = rows // 2
    here = meta[0] * rows
    began = doc_start(meta, here + pl.program_id(0) * half)
    for slot, begin in slots:
        low = began - begin
        for lo, test in ((0, low < half), (half, (low >= half) & (low < rows))):

            @pl.when((begin < here) & test)
            def _(keys=slice(slot * rows + lo, (slot + 1) * rows)):
                work(keys)


def near_kernel(meta, q_ref, k0, v0, k1, v1, k2, v2, k3, v3, *rest):
    acc_ref, total_ref, qx_ref, k_buf, v_buf = rest[-5:]
    rows = k0.shape[0]
    half = rows // 2
    i = pl.program_id(0)
    b = meta[0]
    twin = b + 1 - 2 * (b % 2)
    begins = [b * rows, twin * rows, (b - 2) * rows, (twin - 2) * rows]
    mask_queries(meta, qx_ref, b * rows + i * half, half)

    @pl.when(i == 0)
    def _():
        for slot, (k, v) in enumerate(((k0, v0), (k1, v1), (k2, v2), (k3, v3))):
            fill(meta, k_buf, v_buf, slot, k, v, begins[slot], rows)

    refs = (q_ref, qx_ref, k_buf, v_buf, acc_ref, total_ref)
    for n in range(2):

        @pl.when(i == n)
        def _(n=n):
            shape = (half, (n + 1) * half)
            row = lax.broadcasted_iota(jnp.int32, shape, 0) + n * half
            col = lax.broadcasted_iota(jnp.int32, shape, 1)
            attend(*refs, slice(0, (n + 1) * half), causal=col <= row, add=False)

    add_earlier(
        meta, rows, lambda keys: attend(*refs, keys), [(s, begins[s]) for s in range(1, 4)]
    )


def kv_specs(rows, g, groups, count):
    pair = [
        pl.BlockSpec((rows, HD), lambda i, m: (0, g)),
        pl.BlockSpec((rows, HD), lambda i, m: (0, groups + g)),
    ]
    return pair * count


def near_part(meta, q_soft, kvs, g, *waits):
    rows, cols = q_soft.shape
    groups = kvs[0].shape[1] // (2 * HD)
    width, half, n = cols // groups, rows // 2, len(kvs)
    return pl.pallas_call(
        near_kernel,
        grid_spec=pltpu.PrefetchScalarGridSpec(
            num_scalar_prefetch=1,
            grid=(2,),
            in_specs=[pl.BlockSpec((half, width), lambda i, m: (i, g))]
            + kv_specs(rows, g, groups, n)
            + [pl.BlockSpec(memory_space=pl.ANY)] * len(waits),
            out_specs=[
                pl.BlockSpec((half, width), lambda i, m: (i, 0)),
                pl.BlockSpec((half, HD), lambda i, m: (i, 0)),
            ],
            scratch_shapes=[
                pltpu.VMEM((half, HD), BF),
                pltpu.VMEM((n * rows, 2 * HD), BF),
                pltpu.VMEM((n * rows, 2 * HD), BF),
            ],
        ),
        out_shape=[
            jax.ShapeDtypeStruct((rows, width), F32),
            jax.ShapeDtypeStruct((rows, HD), F32),
        ],
        compiler_params=params(),
        name="attend_near",
    )(meta, q_soft, *[x for kv in kvs for x in (kv, kv)], *waits)


def far_kernel(g, meta, q_ref, acc_in, total_in, k0, v0, k1, v1, e0, e1, e2, e3, *rest):
    out_ref, acc_ref, total_ref, qx_ref, k_buf, v_buf, sem = rest[-7:]
    rows = k0.shape[0]
    half = rows // 2
    heads = q_ref.shape[1] // HD
    groups = e0.shape[1] // (2 * HD)
    i = pl.program_id(0)
    b = meta[0]
    twin = b + 1 - 2 * (b % 2)
    begins = [(b - 4) * rows, (twin - 4) * rows]
    mask_queries(meta, qx_ref, b * rows + i * half, half)
    acc_ref[...] = acc_in[...]
    total_ref[...] = total_in[...]

    @pl.when(i == 0)
    def _():
        for slot, (k, v) in enumerate(((k0, v0), (k1, v1))):
            fill(meta, k_buf, v_buf, slot, k, v, begins[slot], rows)

    refs = (q_ref, qx_ref, k_buf, v_buf, acc_ref, total_ref)
    add_earlier(meta, rows, lambda keys: attend(*refs, keys), list(enumerate(begins)))
    lane = lax.broadcasted_iota(jnp.int32, (half, HD), 1)
    total = total_ref[...]
    fine = ((total > LOW) & (total < HIGH)) | (lane >= heads)
    bad = jnp.max(jnp.where(fine, 0.0, 1.0)) > 0.0
    inverse = 1.0 / total
    for h in range(heads):
        cols = slice(h * HD, (h + 1) * HD)
        out_ref[:, cols] = (acc_ref[:, cols] * inverse[:, h : h + 1]).astype(BF)

    @pl.when(bad)
    def _():
        firsts = [b * rows, twin * rows, (b - 2) * rows, (twin - 2) * rows]
        for slot, (ref, first) in enumerate(zip((e0, e1, e2, e3), firsts)):
            at = slice((slot + 2) * rows, (slot + 3) * rows)
            for buf, off in ((k_buf, g), (v_buf, groups + g)):
                copy = pltpu.make_async_copy(
                    ref.at[:, off * HD : (off + 1) * HD], buf.at[at, :HD], sem
                )
                copy.start()
                copy.wait()
            k_buf[at, HD:] = jnp.where(member(meta, first, rows), 0.0, -BIG).astype(BF)
        spots = [(s + 2, f) for s, f in enumerate(firsts)] + list(enumerate(begins))

        def redo(h, carry):
            cols = pl.ds(pl.multiple_of(h * HD, HD), HD)
            q = jnp.concatenate([q_ref[:, cols], qx_ref[...]], axis=1)
            top = jnp.full((half, 1), -BIG, F32)
            den = jnp.zeros((half, 1), F32)
            num = jnp.zeros((half, HD), F32)
            row = lax.broadcasted_iota(jnp.int32, (half, rows), 0) + (b * rows + i * half)
            col = lax.broadcasted_iota(jnp.int32, (half, rows), 1)
            for slot, first in spots:
                keys = slice(slot * rows, (slot + 1) * rows)
                s = jnp.where(col + first <= row, qk(q, k_buf[keys, :]) * C2, -BIG)
                new = jnp.maximum(top, jnp.max(s, axis=1, keepdims=True))
                p = jnp.exp2(s - new)
                fade = jnp.exp2(top - new)
                den = den * fade + jnp.sum(p, axis=1, keepdims=True)
                num = num * fade + jnp.dot(
                    p.astype(BF), v_buf[keys, :HD], preferred_element_type=F32
                )
                top = new
            out_ref[:, cols] = (num / den).astype(BF)
            return carry

        lax.fori_loop(0, heads, redo, 0)


def far_part(meta, q_soft, acc, total, kvs, spare, g, out, *waits):
    rows, cols = q_soft.shape
    groups = kvs[0].shape[1] // (2 * HD)
    width, half, n = cols // groups, rows // 2, len(kvs)
    slots = n + len(spare)
    extra = list(waits) + ([] if out is None else [out])
    operands = [meta, q_soft, acc, total, *[x for kv in kvs for x in (kv, kv)], *spare, *extra]
    return pl.pallas_call(
        functools.partial(far_kernel, g),
        grid_spec=pltpu.PrefetchScalarGridSpec(
            num_scalar_prefetch=1,
            grid=(2,),
            in_specs=[
                pl.BlockSpec((half, width), lambda i, m: (i, g)),
                pl.BlockSpec((half, width), lambda i, m: (i, 0)),
                pl.BlockSpec((half, HD), lambda i, m: (i, 0)),
            ]
            + kv_specs(rows, g, groups, n)
            + [pl.BlockSpec(memory_space=pl.ANY)] * (len(spare) + len(extra)),
            out_specs=pl.BlockSpec((half, width), lambda i, m: (i, g)),
            scratch_shapes=[
                pltpu.VMEM((half, width), F32),
                pltpu.VMEM((half, HD), F32),
                pltpu.VMEM((half, HD), BF),
                pltpu.VMEM((slots * rows, 2 * HD), BF),
                pltpu.VMEM((slots * rows, 2 * HD), BF),
                pltpu.SemaphoreType.DMA,
            ],
        ),
        out_shape=jax.ShapeDtypeStruct((rows, cols), BF),
        input_output_aliases={} if out is None else {len(operands) - 1: 0},
        compiler_params=params(),
        name="attend_far",
    )(*operands)


def after(value, *others):
    return lax.optimization_barrier((value, *others))[0]


def shards(q_lin, k_lin, v_lin, lin_gain, q_soft, k_soft, v_soft, doc_lengths):
    rows = q_lin.shape[0]
    peers = lax.axis_size("ctx")
    rings = lax.axis_size("head")
    next_chip = [(i, (i + 2) % peers) for i in range(peers)]
    twins = [(i, i ^ 1) for i in range(peers)]

    def forward(x):
        return lax.ppermute(x, "ctx", next_chip)

    def swap(x):
        return lax.ppermute(x, "ctx", twins)

    def shift(x, by):
        return lax.ppermute(x, "head", [(i, (i + by) % rings) for i in range(rings)])

    meta = jnp.concatenate([lax.axis_index("ctx").astype(jnp.int32)[None], doc_lengths])
    kv = joined(k_soft, v_soft)
    kv_one = forward(kv)
    kv_twin = swap(kv)

    keep, send = local_state(after(meta, kv), k_lin, v_lin)
    got = swap(send)
    inside = inside_part(after(meta, send), q_lin, k_lin, v_lin)
    chip = chip_state(meta, keep, after(got, inside), rows)
    one = forward(chip)

    kv_one = after(kv_one, chip)
    kv_two = forward(kv_one)
    kv_one_twin = swap(kv_one)
    near_kvs = (kv, kv_twin, kv_one, kv_one_twin)
    acc0, total0 = near_part(meta, q_soft, near_kvs, 0)
    two = forward(after(one, acc0))
    acc1, total1 = near_part(after(meta, acc0), q_soft, near_kvs, 1)

    mine, pay = entering(meta, one, after(two, acc1), keep, got, rows)
    other = swap(pay)
    kv_two_twin = swap(after(kv_two, acc1))
    far_kvs = (kv_two, kv_two_twin)
    mix, sums = carried_part(meta, q_lin, inside, mine, other)
    sums_one = shift(sums, 1)
    attn = far_part(after(meta, sums), q_soft, acc0, total0, far_kvs, near_kvs, 0, None)
    pair = sums + after(sums_one, attn)
    pair_two = shift(pair, 2)
    attn = far_part(after(meta, pair), q_soft, acc1, total1, far_kvs, near_kvs, 1, attn)
    lin_out = norm_part(mix, (pair, after(pair_two, attn)), lin_gain.reshape(1, -1))
    return lin_out, attn


def solution(mesh):
    return jax.shard_map(
        shards,
        mesh=mesh,
        in_specs=(
            P("ctx", "head"),
            P("ctx", "head"),
            P("ctx", "head"),
            P("head"),
            P("ctx", "head"),
            P("ctx", "head"),
            P("ctx", "head"),
            P(),
        ),
        out_specs=(P("ctx", "head"), P("ctx", "head")),
        check_vma=False,
    )
```

```python
import math

import jax
import jax.numpy as jnp
from jax import lax
from jax.experimental import pallas as pl
from jax.experimental.pallas import tpu as pltpu
from jax.sharding import PartitionSpec as P

H = 64
HD = 128
EPS = 1e-05
BIG = 1e30
AT_ONCE = 4
LOW = 2.0**-60
HIGH = 2.0**100
C2 = math.log2(math.e) / math.sqrt(HD)
BF = jnp.bfloat16
F32 = jnp.float32
VMEM_LIMIT = 32 * 1024 * 1024
INSIDE_LIMIT = 60 * 1024 * 1024


class Meta:
    def __init__(self, place, lengths):
        self.place, self.lengths = place, lengths
        self.shape = (1 + lengths.shape[0],)

    def __getitem__(self, i):
        return self.place[0] if i == 0 else self.lengths[i - 1]


def with_meta(kernel, *leading):
    def wrapped(place, lengths, *refs):
        kernel(*leading, Meta(place, lengths), *refs)

    return wrapped


def doc_start(meta, pos):
    total, start = jnp.int32(0), jnp.int32(0)
    for d in range(1, meta.shape[0]):
        start = jnp.where(total <= pos, total, start)
        total = total + meta[d]
    return start


def doc_end(meta, pos):
    total, end = jnp.int32(0), jnp.int32(0)
    for d in range(1, meta.shape[0]):
        end = jnp.where(total <= pos, total + meta[d], end)
        total = total + meta[d]
    return end


def doc_rows(meta):
    lane = lax.broadcasted_iota(jnp.int32, (1, HD), 1)
    start = jnp.full((1, HD), 1 << 30, jnp.int32)
    end = jnp.full((1, HD), 1 << 30, jnp.int32)
    total = jnp.int32(0)
    for d in range(1, meta.shape[0]):
        start = jnp.where(lane == d - 1, total, start)
        total = total + meta[d]
        end = jnp.where(lane == d - 1, total, end)
    return start, end


def member(meta, first, count):
    start, end = doc_rows(meta)
    pos = first + lax.broadcasted_iota(jnp.int32, (count, HD), 0)
    return (pos >= start) & (pos < end)


def params(limit=VMEM_LIMIT):
    return pltpu.CompilerParams(vmem_limit_bytes=limit)


def qk(q, k):
    return lax.dot_general(q, k, (((1,), (1,)), ((), ())), preferred_element_type=F32)


def local_kernel(meta, q_ref, k_ref, v_ref, state_ref, out_ref, mask_ref):
    rows = q_ref.shape[0]
    half = rows // 2
    first = meta[0] * rows
    tail = doc_start(meta, first + rows - 1) - first
    live = lax.broadcasted_iota(jnp.int32, (rows, 2 * HD), 0) >= tail

    @pl.when(pl.program_id(0) == 0)
    def _():
        start, _ = doc_rows(meta)
        pos = first + lax.broadcasted_iota(jnp.int32, (rows, HD), 0)
        began = jnp.max(jnp.where(pos >= start, start, -1), axis=1, keepdims=True) - first
        row = lax.broadcasted_iota(jnp.int32, (rows, rows), 0)
        col = lax.broadcasted_iota(jnp.int32, (rows, rows), 1)
        mask_ref[...] = jnp.where((col <= row) & (col >= began), 1.0, 0.0).astype(BF)

    for j in range(0, q_ref.shape[1] // HD, 2):
        pair = slice(j * HD, (j + 2) * HD)
        k = jnp.where(live, k_ref[:, pair], jnp.zeros((rows, 2 * HD), BF))
        s = lax.dot_general(
            k, v_ref[:, pair], (((0,), (0,)), ((), ())), preferred_element_type=F32
        ).astype(BF)
        for e in range(2):
            part = slice(e * HD, (e + 1) * HD)
            cols = slice((j + e) * HD, (j + e + 1) * HD)
            state_ref[cols, :] = s[part, part]
            for i in range(2):
                at, upto = slice(i * half, (i + 1) * half), slice(0, (i + 1) * half)
                w = qk(q_ref[at, cols], k_ref[upto, cols]).astype(BF) * mask_ref[at, upto]
                o = jnp.dot(w, v_ref[upto, pair], preferred_element_type=F32)
                out_ref[at, cols] = o[:, part].astype(BF)


def local_part(meta, q_lin, k_lin, v_lin, other, steps=2):
    rows, cols = q_lin.shape
    block = cols // (2 * steps)
    spec = pl.BlockSpec((rows, block), lambda i, m, n: (0, steps * ((m[0] + other) % 2) + i))
    return pl.pallas_call(
        with_meta(local_kernel),
        grid_spec=pltpu.PrefetchScalarGridSpec(
            num_scalar_prefetch=2,
            grid=(steps,),
            in_specs=[spec] * 3,
            out_specs=[
                pl.BlockSpec((block, HD), lambda i, m, n: (i, 0)),
                pl.BlockSpec((rows, block), lambda i, m, n: (0, i)),
            ],
            scratch_shapes=[pltpu.VMEM((rows, rows), BF)],
        ),
        out_shape=[
            jax.ShapeDtypeStruct((cols // 2, HD), BF),
            jax.ShapeDtypeStruct((rows, cols // 2), BF),
        ],
        compiler_params=params(61 * 1024 * 1024),
        name="local",
    )(*meta, q_lin, k_lin, v_lin)


def state_kernel(meta, k_ref, v_ref, state_ref):
    rows = k_ref.shape[0]
    first = meta[0] * rows
    tail = doc_start(meta, first + rows - 1) - first
    live = lax.broadcasted_iota(jnp.int32, (rows, 2 * HD), 0) >= tail
    for j in range(0, k_ref.shape[1] // HD, 2):
        pair = slice(j * HD, (j + 2) * HD)
        k = jnp.where(live, k_ref[:, pair], jnp.zeros((rows, 2 * HD), BF))
        s = lax.dot_general(
            k, v_ref[:, pair], (((0,), (0,)), ((), ())), preferred_element_type=F32
        ).astype(BF)
        for e in range(2):
            part = slice(e * HD, (e + 1) * HD)
            state_ref[(j + e) * HD : (j + e + 1) * HD, :] = s[part, part]


def state_part(meta, k_lin, v_lin, steps=2):
    rows, cols = k_lin.shape
    block = cols // (2 * steps)
    spec = pl.BlockSpec((rows, block), lambda i, m, n: (0, steps * (m[0] % 2) + i))
    return pl.pallas_call(
        with_meta(state_kernel),
        grid_spec=pltpu.PrefetchScalarGridSpec(
            num_scalar_prefetch=2,
            grid=(steps,),
            in_specs=[spec] * 2,
            out_specs=pl.BlockSpec((block, HD), lambda i, m, n: (i, 0)),
        ),
        out_shape=jax.ShapeDtypeStruct((cols // 2, HD), BF),
        compiler_params=params(62 * 1024 * 1024),
        name="state",
    )(*meta, k_lin, v_lin)


def inside_kernel(meta, q_ref, k_ref, v_ref, out_ref, mask_ref):
    rows = q_ref.shape[0]
    half = rows // 2
    first = meta[0] * rows

    @pl.when(pl.program_id(0) == 0)
    def _():
        start, _ = doc_rows(meta)
        pos = first + lax.broadcasted_iota(jnp.int32, (rows, HD), 0)
        began = jnp.max(jnp.where(pos >= start, start, -1), axis=1, keepdims=True) - first
        row = lax.broadcasted_iota(jnp.int32, (rows, rows), 0)
        col = lax.broadcasted_iota(jnp.int32, (rows, rows), 1)
        mask_ref[...] = jnp.where((col <= row) & (col >= began), 1.0, 0.0).astype(BF)

    for j in range(q_ref.shape[1] // HD):
        cols = slice(j * HD, (j + 1) * HD)
        pair = slice((j - j % 2) * HD, (j - j % 2 + 2) * HD)
        part = slice((j % 2) * HD, (j % 2 + 1) * HD)
        for i in range(2):
            at, upto = slice(i * half, (i + 1) * half), slice(0, (i + 1) * half)
            w = qk(q_ref[at, cols], k_ref[upto, cols]).astype(BF) * mask_ref[at, upto]
            o = jnp.dot(w, v_ref[upto, pair], preferred_element_type=F32)
            out_ref[at, cols] = o[:, part].astype(BF)


def inside_part(meta, q_lin, k_lin, v_lin, other, steps=2):
    rows, cols = q_lin.shape
    block = cols // (2 * steps)
    spec = pl.BlockSpec((rows, block), lambda i, m, n: (0, steps * ((m[0] + other) % 2) + i))
    return pl.pallas_call(
        with_meta(inside_kernel),
        grid_spec=pltpu.PrefetchScalarGridSpec(
            num_scalar_prefetch=2,
            grid=(steps,),
            in_specs=[spec] * 3,
            out_specs=pl.BlockSpec((rows, block), lambda i, m, n: (0, i)),
            scratch_shapes=[pltpu.VMEM((rows, rows), BF)],
        ),
        out_shape=jax.ShapeDtypeStruct((rows, cols // 2), BF),
        compiler_params=params(INSIDE_LIMIT),
        name="inside",
    )(*meta, q_lin, k_lin, v_lin)


def chip_kernel(rows, meta, own_ref, got_ref, out_ref):
    b = meta[0]
    second = b - b % 2 + 1
    whole = (doc_start(meta, second * rows + rows - 1) < second * rows).astype(F32)
    odd = (b % 2).astype(F32)
    scale_own = odd + (1.0 - odd) * whole
    scale_got = (1.0 - odd) + odd * whole
    out_ref[...] = (scale_own * own_ref[...].astype(F32) + scale_got * got_ref[...].astype(F32)).astype(BF)


def chip_state(meta, own, got, rows):
    return pl.pallas_call(
        with_meta(chip_kernel, rows),
        in_specs=[pl.BlockSpec(memory_space=pltpu.SMEM)] * 2 + [pl.BlockSpec(memory_space=pltpu.VMEM)] * 2,
        out_specs=pl.BlockSpec(memory_space=pltpu.VMEM),
        out_shape=jax.ShapeDtypeStruct(own.shape, BF),
        compiler_params=params(),
        name="chip_state",
    )(*meta, own, got)


def enter_kernel(rows, meta, one_ref, two_ref, own_ref, got_ref, mine_ref, pay_ref):
    b = meta[0]
    first = b - b % 2
    before = first * rows - 2 * rows
    chained = (doc_start(meta, first * rows - 1) < before).astype(F32)
    passes = (doc_start(meta, first * rows + rows - 1) < first * rows).astype(F32)
    odd = (b % 2).astype(F32)
    even = 1.0 - odd
    state = one_ref[...].astype(F32) + chained * two_ref[...].astype(F32)
    mine_ref[...] = ((even + odd * passes) * state + odd * got_ref[...].astype(F32)).astype(BF)
    pay_ref[...] = ((odd + even * passes) * state + even * own_ref[...].astype(F32)).astype(BF)


def entering(meta, one, two, own, got, rows):
    return pl.pallas_call(
        with_meta(enter_kernel, rows),
        in_specs=[pl.BlockSpec(memory_space=pltpu.SMEM)] * 2 + [pl.BlockSpec(memory_space=pltpu.VMEM)] * 4,
        out_specs=[pl.BlockSpec(memory_space=pltpu.VMEM)] * 2,
        out_shape=[jax.ShapeDtypeStruct(own.shape, BF)] * 2,
        compiler_params=params(),
        name="entering",
    )(*meta, one, two, own, got)


def carried_kernel(meta, q_ref, in_mine, in_other, mine_ref, other_ref, mix_ref, sum_ref, acc_ref):
    i = pl.program_id(0)
    rows = q_ref.shape[0]
    b = meta[0]
    first = b * rows
    reach = jnp.where(doc_start(meta, first) < first, doc_end(meta, first) - first, 0)
    row = lax.broadcasted_iota(jnp.int32, (rows, 2 * HD), 0)
    live = row < reach
    none = jnp.zeros((HD, HD), BF)

    def work(in_ref, state_ref, squares):
        for j in range(0, q_ref.shape[1] // HD, 2):
            cols = slice(j * HD, (j + 2) * HD)
            one, two = (state_ref[(j + e) * HD : (j + e + 1) * HD, :] for e in range(2))
            state = jnp.concatenate(
                [jnp.concatenate([one, none], axis=1), jnp.concatenate([none, two], axis=1)], axis=0
            )
            term = jnp.dot(q_ref[:, cols], state, preferred_element_type=F32)
            mix = in_ref[:, cols].astype(F32) + jnp.where(live, term, 0.0)
            square = mix * mix
            squares = squares + (square[:, :HD] + square[:, HD:])
            mix_ref[:, cols] = mix.astype(BF)
        return squares

    @pl.when(i == 0)
    def _():
        acc_ref[...] = work(in_mine, mine_ref, jnp.zeros((rows, HD), F32))

    @pl.when(i == 1)
    def _():
        squares = work(in_other, other_ref, acc_ref[...])
        sum_ref[...] = jnp.sum(squares.T, axis=0, keepdims=True)


def carried_part(meta, q_lin, in_mine, in_other, mine, other):
    rows, cols = q_lin.shape
    spec = pl.BlockSpec((rows, cols // 2), lambda i, m, n: (0, (i + m[0]) % 2))
    part = pl.BlockSpec((rows, cols // 2), lambda i, m, n: (0, 0))
    whole = pl.BlockSpec(mine.shape, lambda i, m, n: (0, 0))
    return pl.pallas_call(
        with_meta(carried_kernel),
        grid_spec=pltpu.PrefetchScalarGridSpec(
            num_scalar_prefetch=2,
            grid=(2,),
            in_specs=[spec, part, part, whole, whole],
            out_specs=[spec, pl.BlockSpec((1, rows), lambda i, m, n: (0, 0))],
            scratch_shapes=[pltpu.VMEM((rows, HD), F32)],
        ),
        out_shape=[jax.ShapeDtypeStruct((rows, cols), BF), jax.ShapeDtypeStruct((1, rows), F32)],
        compiler_params=params(),
        name="carried",
    )(*meta, q_lin, in_mine, in_other, mine, other)


def norm_kernel(mix_ref, a_ref, b_ref, gain_ref, out_ref):
    rows = mix_ref.shape[0]
    total = a_ref[...] + b_ref[...]
    inv = lax.rsqrt(total / (H * HD) + EPS)
    inv = jnp.broadcast_to(inv, (HD, rows)).T
    for j in range(mix_ref.shape[1] // HD):
        cols = slice(j * HD, (j + 1) * HD)
        out_ref[:, cols] = (mix_ref[:, cols].astype(F32) * inv * gain_ref[:, cols]).astype(BF)


def norm_part(mix, sums, gain, steps=2):
    rows, cols = mix.shape
    spec = pl.BlockSpec((rows, cols // steps), lambda i: (0, i))
    one = pl.BlockSpec((1, rows), lambda i: (0, 0))
    return pl.pallas_call(
        norm_kernel,
        grid=(steps,),
        in_specs=[spec, one, one, pl.BlockSpec((1, cols // steps), lambda i: (0, i))],
        out_specs=spec,
        out_shape=jax.ShapeDtypeStruct((rows, cols), BF),
        compiler_params=params(),
        name="norm",
    )(mix, *sums, gain)


def fill(meta, k_buf, v_buf, slot, k_ref, v_ref, first, count):
    at = pl.ds(pl.multiple_of(slot * count, count), count)
    k_buf[at, :HD] = k_ref[...]
    k_buf[at, HD:] = jnp.where(member(meta, first, count), 0.0, -BIG).astype(BF)
    v_buf[at, :HD] = v_ref[...]
    v_buf[at, HD:] = jnp.ones((count, HD), BF)


def mask_queries(meta, qx_ref, first, count):
    qx_ref[...] = jnp.where(member(meta, first, count), 1.0, 0.0).astype(BF)


def join_kernel(k_ref, v_ref, out_ref):
    width = k_ref.shape[1]
    out_ref[:, :width] = k_ref[...]
    out_ref[:, width:] = v_ref[...]


def joined(k, v):
    rows, width = k.shape
    return pl.pallas_call(
        join_kernel,
        in_specs=[pl.BlockSpec(memory_space=pltpu.VMEM)] * 2,
        out_specs=pl.BlockSpec(memory_space=pltpu.VMEM),
        out_shape=jax.ShapeDtypeStruct((rows, 2 * width), k.dtype),
        compiler_params=params(62 * 1024 * 1024),
        name="join",
    )(k, v)


def attend(q_ref, qx_ref, k_buf, v_buf, acc_ref, total_ref, keys, last):
    half = q_ref.shape[0]
    lane = lax.broadcasted_iota(jnp.int32, total_ref.shape, 1)
    packed = jnp.zeros(total_ref.shape, F32) if last else total_ref[...]
    if last:
        row = lax.broadcasted_iota(jnp.int32, (half, half), 0)
        col = lax.broadcasted_iota(jnp.int32, (half, half), 1)
        causal = col <= row

    def some(step, packed):
        for e in range(AT_ONCE):
            h = step * AT_ONCE + e
            cols = pl.ds(pl.multiple_of(h * HD, HD), HD)
            q = jnp.concatenate([q_ref[:, cols], qx_ref[...]], axis=1)
            p = jnp.exp2(qk(q, k_buf[keys, :]) * C2)
            if last:
                own = jnp.where(causal, p[:, -half:], 0.0)
                p = own if p.shape[1] == half else jnp.concatenate([p[:, :-half], own], axis=1)
            o = jnp.dot(p.astype(BF), v_buf[keys, :], preferred_element_type=F32)
            if last:
                acc_ref[:, cols] = o[:, :HD]
            else:
                acc_ref[:, cols] += o[:, :HD]
            packed = packed + jnp.where(lane == h, o[:, HD:], 0.0)
        return packed

    total_ref[...] = lax.fori_loop(0, q_ref.shape[1] // (HD * AT_ONCE), some, packed)


def each_length(start, end, most, unit, work):
    for count in range(1, most + 1):

        @pl.when(end - start == count)
        def _(count=count):
            work(pl.ds(pl.multiple_of(start * unit, unit), count * unit))


def near_kernel(meta, q_ref, k0, v0, k1, v1, k2, v2, k3, v3, *rest):
    acc_ref, total_ref, qx_ref, k_buf, v_buf = rest[-5:]
    rows = k0.shape[0]
    half = rows // 2
    i = pl.program_id(0)
    b = meta[0]
    odd = b % 2
    mask_queries(meta, qx_ref, b * rows + i * half, half)
    oldest = (b - 3) * rows

    @pl.when(i == 0)
    def _():
        spots = [(k0, v0, 3), (k2, v2, 1), (k3, v3, 2 - 2 * odd)]
        for k, v, slot in spots:
            fill(meta, k_buf, v_buf, slot, k, v, oldest + slot * rows, rows)

        @pl.when(odd == 1)
        def _():
            fill(meta, k_buf, v_buf, 2, k1, v1, oldest + 2 * rows, rows)

    began = doc_start(meta, b * rows + i * half) - oldest
    start = jnp.maximum(began, 2 * half * (1 - odd)) // half
    each_length(
        start,
        7 + i,
        8,
        half,
        lambda keys: attend(q_ref, qx_ref, k_buf, v_buf, acc_ref, total_ref, keys, True),
    )


def kv_specs(rows, g, groups, count):
    pair = [
        pl.BlockSpec((rows, HD), lambda i, m, n: (0, g)),
        pl.BlockSpec((rows, HD), lambda i, m, n: (0, groups + g)),
    ]
    return pair * count


def near_part(meta, q_soft, kvs, g, *waits):
    rows, cols = q_soft.shape
    groups = kvs[0].shape[1] // (2 * HD)
    width, half, n = cols // groups, rows // 2, len(kvs)
    return pl.pallas_call(
        with_meta(near_kernel),
        grid_spec=pltpu.PrefetchScalarGridSpec(
            num_scalar_prefetch=2,
            grid=(2,),
            in_specs=[pl.BlockSpec((half, width), lambda i, m, n: (i, g))]
            + kv_specs(rows, g, groups, n)
            + [pl.BlockSpec(memory_space=pl.ANY)] * len(waits),
            out_specs=[
                pl.BlockSpec((half, width), lambda i, m, n: (i, 0)),
                pl.BlockSpec((half, HD), lambda i, m, n: (i, 0)),
            ],
            scratch_shapes=[
                pltpu.VMEM((half, HD), BF),
                pltpu.VMEM((n * rows, 2 * HD), BF),
                pltpu.VMEM((n * rows, 2 * HD), BF),
            ],
        ),
        out_shape=[
            jax.ShapeDtypeStruct((rows, width), F32),
            jax.ShapeDtypeStruct((rows, HD), F32),
        ],
        compiler_params=params(),
        name="attend_near",
    )(*meta, q_soft, *[x for kv in kvs for x in (kv, kv)], *waits)


def far_kernel(g, meta, q_ref, acc_in, total_in, k0, v0, k1, v1, e0, e1, e2, e3, *rest):
    out_ref, acc_ref, total_ref, qx_ref, k_buf, v_buf, sem = rest[-7:]
    rows = k0.shape[0]
    half = rows // 2
    heads = q_ref.shape[1] // HD
    groups = e0.shape[1] // (2 * HD)
    i = pl.program_id(0)
    b = meta[0]
    twin = b + 1 - 2 * (b % 2)
    begins = [(b - 4) * rows, (twin - 4) * rows]
    mask_queries(meta, qx_ref, b * rows + i * half, half)
    acc_ref[...] = acc_in[...]
    total_ref[...] = total_in[...]
    began = doc_start(meta, b * rows + i * half) - begins[0]
    start = jnp.maximum(began, 0) // half
    end = 4 - 2 * (b % 2)

    @pl.when((i == 0) & (start < end))
    def _():
        for slot, (k, v) in enumerate(((k0, v0), (k1, v1))):
            fill(meta, k_buf, v_buf, slot, k, v, begins[slot], rows)

    each_length(
        start,
        end,
        4,
        half,
        lambda keys: attend(q_ref, qx_ref, k_buf, v_buf, acc_ref, total_ref, keys, False),
    )
    lane = lax.broadcasted_iota(jnp.int32, (half, HD), 1)
    total = total_ref[...]
    fine = ((total > LOW) & (total < HIGH)) | (lane >= heads)
    bad = jnp.max(jnp.where(fine, 0.0, 1.0)) > 0.0
    inverse = 1.0 / total
    for h in range(heads):
        cols = slice(h * HD, (h + 1) * HD)
        out_ref[:, cols] = (acc_ref[:, cols] * inverse[:, h : h + 1]).astype(BF)

    @pl.when(bad)
    def _():
        firsts = [b * rows, twin * rows, (b - 2) * rows, (twin - 2) * rows]
        for slot, (k, v) in enumerate(((k0, v0), (k1, v1))):
            fill(meta, k_buf, v_buf, slot, k, v, begins[slot], rows)
        for slot, (ref, first) in enumerate(zip((e0, e1, e2, e3), firsts)):
            at = slice((slot + 2) * rows, (slot + 3) * rows)
            for buf, off in ((k_buf, g), (v_buf, groups + g)):
                copy = pltpu.make_async_copy(
                    ref.at[:, off * HD : (off + 1) * HD], buf.at[at, :HD], sem
                )
                copy.start()
                copy.wait()
            k_buf[at, HD:] = jnp.where(member(meta, first, rows), 0.0, -BIG).astype(BF)
        spots = [(s + 2, f) for s, f in enumerate(firsts)] + list(enumerate(begins))

        def redo(h, carry):
            cols = pl.ds(pl.multiple_of(h * HD, HD), HD)
            q = jnp.concatenate([q_ref[:, cols], qx_ref[...]], axis=1)
            top = jnp.full((half, 1), -BIG, F32)
            den = jnp.zeros((half, 1), F32)
            num = jnp.zeros((half, HD), F32)
            row = lax.broadcasted_iota(jnp.int32, (half, rows), 0) + (b * rows + i * half)
            col = lax.broadcasted_iota(jnp.int32, (half, rows), 1)
            for slot, first in spots:
                keys = slice(slot * rows, (slot + 1) * rows)
                s = jnp.where(col + first <= row, qk(q, k_buf[keys, :]) * C2, -BIG)
                new = jnp.maximum(top, jnp.max(s, axis=1, keepdims=True))
                p = jnp.exp2(s - new)
                fade = jnp.exp2(top - new)
                den = den * fade + jnp.sum(p, axis=1, keepdims=True)
                num = num * fade + jnp.dot(
                    p.astype(BF), v_buf[keys, :HD], preferred_element_type=F32
                )
                top = new
            out_ref[:, cols] = (num / den).astype(BF)
            return carry

        lax.fori_loop(0, heads, redo, 0)


def far_part(meta, q_soft, acc, total, kvs, spare, g, out, *waits):
    rows, cols = q_soft.shape
    groups = kvs[0].shape[1] // (2 * HD)
    width, half, n = cols // groups, rows // 2, len(kvs)
    slots = n + len(spare)
    extra = list(waits) + ([] if out is None else [out])
    operands = [*meta, q_soft, acc, total, *[x for kv in kvs for x in (kv, kv)], *spare, *extra]
    return pl.pallas_call(
        with_meta(far_kernel, g),
        grid_spec=pltpu.PrefetchScalarGridSpec(
            num_scalar_prefetch=2,
            grid=(2,),
            in_specs=[
                pl.BlockSpec((half, width), lambda i, m, n: (i, g)),
                pl.BlockSpec((half, width), lambda i, m, n: (i, 0)),
                pl.BlockSpec((half, HD), lambda i, m, n: (i, 0)),
            ]
            + kv_specs(rows, g, groups, n)
            + [pl.BlockSpec(memory_space=pl.ANY)] * (len(spare) + len(extra)),
            out_specs=pl.BlockSpec((half, width), lambda i, m, n: (i, g)),
            scratch_shapes=[
                pltpu.VMEM((half, width), F32),
                pltpu.VMEM((half, HD), F32),
                pltpu.VMEM((half, HD), BF),
                pltpu.VMEM((slots * rows, 2 * HD), BF),
                pltpu.VMEM((slots * rows, 2 * HD), BF),
                pltpu.SemaphoreType.DMA,
            ],
        ),
        out_shape=jax.ShapeDtypeStruct((rows, cols), BF),
        input_output_aliases={} if out is None else {len(operands) - 1: 0},
        compiler_params=params(),
        name="attend_far",
    )(*operands)


def after(value, *others):
    return lax.optimization_barrier((value, *others))[0]


def shards(q_lin, k_lin, v_lin, lin_gain, q_soft, k_soft, v_soft, doc_lengths):
    rows = q_lin.shape[0]
    peers = lax.axis_size("ctx")
    rings = lax.axis_size("head")
    next_chip = [(i, (i + 2) % peers) for i in range(peers)]
    twins = [(i, i ^ 1) for i in range(peers)]

    def forward(x):
        return lax.ppermute(x, "ctx", next_chip)

    def swap(x):
        return lax.ppermute(x, "ctx", twins)

    def shift(x, by):
        return lax.ppermute(x, "head", [(i, (i + by) % rings) for i in range(rings)])

    meta = (lax.axis_index("ctx").astype(jnp.int32).reshape(1), doc_lengths)
    kv = joined(k_soft, v_soft)
    kv_one = forward(kv)
    kv_twin = swap(kv)

    send, in_other = local_part(after(meta, kv), q_lin, k_lin, v_lin, 1)
    got = swap(send)
    keep = state_part(after(meta, send), k_lin, v_lin)
    chip = chip_state(after(meta, keep), keep, got, rows)
    one = forward(chip)
    in_mine = inside_part(after(meta, chip), q_lin, k_lin, v_lin, 0)

    kv_one = after(kv_one, chip)
    kv_one_twin = swap(kv_one)
    two = forward(after(one, in_mine))
    kv_two = forward(after(kv_one, one, in_mine))
    near_kvs = (kv, kv_twin, kv_one, kv_one_twin)
    acc0, total0 = near_part(after(meta, in_mine, one), q_soft, near_kvs, 0)
    acc1, total1 = near_part(after(meta, acc0), q_soft, near_kvs, 1)

    mine, pay = entering(meta, one, after(two, acc1), keep, got, rows)
    other = swap(pay)
    kv_two_twin = swap(after(kv_two, acc1))
    far_kvs = (kv_two, kv_two_twin)
    mix, sums = carried_part(meta, q_lin, in_mine, in_other, mine, other)
    sums_one = shift(sums, 1)
    attn = far_part(after(meta, sums), q_soft, acc0, total0, far_kvs, near_kvs, 0, None)
    pair = sums + after(sums_one, attn)
    pair_two = shift(pair, 2)
    attn = far_part(after(meta, pair), q_soft, acc1, total1, far_kvs, near_kvs, 1, attn)
    lin_out = norm_part(mix, (pair, after(pair_two, attn)), lin_gain.reshape(1, -1))
    return lin_out, attn


def solution(mesh):
    return jax.shard_map(
        shards,
        mesh=mesh,
        in_specs=(
            P("ctx", "head"),
            P("ctx", "head"),
            P("ctx", "head"),
            P("head"),
            P("ctx", "head"),
            P("ctx", "head"),
            P("ctx", "head"),
            P(),
        ),
        out_specs=(P("ctx", "head"), P("ctx", "head")),
        check_vma=False,
    )
```

```python
import math

import jax
import jax.numpy as jnp
from jax import lax
from jax.experimental import pallas as pl
from jax.experimental.pallas import tpu as pltpu
from jax.sharding import PartitionSpec as P

H = 64
HD = 128
EPS = 1e-05
BIG = 1e30
AT_ONCE = 4
LOW = 2.0**-60
HIGH = 2.0**100
C2 = math.log2(math.e) / math.sqrt(HD)
BF = jnp.bfloat16
F32 = jnp.float32
VMEM_LIMIT = 32 * 1024 * 1024
INSIDE_LIMIT = 60 * 1024 * 1024


class Meta:
    def __init__(self, place, lengths):
        self.place, self.lengths = place, lengths
        self.shape = (1 + lengths.shape[0],)

    def __getitem__(self, i):
        return self.place[0] if i == 0 else self.lengths[i - 1]


def with_meta(kernel, *leading):
    def wrapped(place, lengths, *refs):
        kernel(*leading, Meta(place, lengths), *refs)

    return wrapped


def doc_start(meta, pos):
    total, start = jnp.int32(0), jnp.int32(0)
    for d in range(1, meta.shape[0]):
        start = jnp.where(total <= pos, total, start)
        total = total + meta[d]
    return start


def doc_end(meta, pos):
    total, end = jnp.int32(0), jnp.int32(0)
    for d in range(1, meta.shape[0]):
        end = jnp.where(total <= pos, total + meta[d], end)
        total = total + meta[d]
    return end


def doc_rows(meta):
    lane = lax.broadcasted_iota(jnp.int32, (1, HD), 1)
    start = jnp.full((1, HD), 1 << 30, jnp.int32)
    end = jnp.full((1, HD), 1 << 30, jnp.int32)
    total = jnp.int32(0)
    for d in range(1, meta.shape[0]):
        start = jnp.where(lane == d - 1, total, start)
        total = total + meta[d]
        end = jnp.where(lane == d - 1, total, end)
    return start, end


def member(docs, first, count):
    start, end = docs
    pos = first + lax.broadcasted_iota(jnp.int32, (count, HD), 0)
    return (pos >= start) & (pos < end)


def params(limit=VMEM_LIMIT):
    return pltpu.CompilerParams(vmem_limit_bytes=limit)


def qk(q, k):
    return lax.dot_general(q, k, (((1,), (1,)), ((), ())), preferred_element_type=F32)


def local_kernel(meta, q_ref, k_ref, v_ref, state_ref, out_ref, mask_ref):
    rows = q_ref.shape[0]
    half = rows // 2
    first = meta[0] * rows
    tail = doc_start(meta, first + rows - 1) - first
    live = lax.broadcasted_iota(jnp.int32, (rows, 2 * HD), 0) >= tail

    @pl.when(pl.program_id(0) == 0)
    def _():
        start, _ = doc_rows(meta)
        pos = first + lax.broadcasted_iota(jnp.int32, (rows, HD), 0)
        began = jnp.max(jnp.where(pos >= start, start, -1), axis=1, keepdims=True) - first
        row = lax.broadcasted_iota(jnp.int32, (rows, rows), 0)
        col = lax.broadcasted_iota(jnp.int32, (rows, rows), 1)
        mask_ref[...] = jnp.where((col <= row) & (col >= began), 1.0, 0.0).astype(BF)

    for j in range(0, q_ref.shape[1] // HD, 2):
        pair = slice(j * HD, (j + 2) * HD)
        k = jnp.where(live, k_ref[:, pair], jnp.zeros((rows, 2 * HD), BF))
        s = lax.dot_general(
            k, v_ref[:, pair], (((0,), (0,)), ((), ())), preferred_element_type=F32
        ).astype(BF)
        for e in range(2):
            part = slice(e * HD, (e + 1) * HD)
            cols = slice((j + e) * HD, (j + e + 1) * HD)
            state_ref[cols, :] = s[part, part]
            for i in range(2):
                at, upto = slice(i * half, (i + 1) * half), slice(0, (i + 1) * half)
                w = qk(q_ref[at, cols], k_ref[upto, cols]).astype(BF) * mask_ref[at, upto]
                o = jnp.dot(w, v_ref[upto, pair], preferred_element_type=F32)
                out_ref[at, cols] = o[:, part].astype(BF)


def local_part(meta, q_lin, k_lin, v_lin, other, steps=2):
    rows, cols = q_lin.shape
    block = cols // (2 * steps)
    spec = pl.BlockSpec((rows, block), lambda i, m, n: (0, steps * ((m[0] + other) % 2) + i))
    return pl.pallas_call(
        with_meta(local_kernel),
        grid_spec=pltpu.PrefetchScalarGridSpec(
            num_scalar_prefetch=2,
            grid=(steps,),
            in_specs=[spec] * 3,
            out_specs=[
                pl.BlockSpec((block, HD), lambda i, m, n: (i, 0)),
                pl.BlockSpec((rows, block), lambda i, m, n: (0, i)),
            ],
            scratch_shapes=[pltpu.VMEM((rows, rows), BF)],
        ),
        out_shape=[
            jax.ShapeDtypeStruct((cols // 2, HD), BF),
            jax.ShapeDtypeStruct((rows, cols // 2), BF),
        ],
        compiler_params=params(61 * 1024 * 1024),
        name="local",
    )(*meta, q_lin, k_lin, v_lin)


def state_kernel(meta, k_ref, v_ref, state_ref):
    rows = k_ref.shape[0]
    first = meta[0] * rows
    tail = doc_start(meta, first + rows - 1) - first
    live = lax.broadcasted_iota(jnp.int32, (rows, 2 * HD), 0) >= tail
    for j in range(0, k_ref.shape[1] // HD, 2):
        pair = slice(j * HD, (j + 2) * HD)
        k = jnp.where(live, k_ref[:, pair], jnp.zeros((rows, 2 * HD), BF))
        s = lax.dot_general(
            k, v_ref[:, pair], (((0,), (0,)), ((), ())), preferred_element_type=F32
        ).astype(BF)
        for e in range(2):
            part = slice(e * HD, (e + 1) * HD)
            state_ref[(j + e) * HD : (j + e + 1) * HD, :] = s[part, part]


def state_part(meta, k_lin, v_lin, steps=2):
    rows, cols = k_lin.shape
    block = cols // (2 * steps)
    spec = pl.BlockSpec((rows, block), lambda i, m, n: (0, steps * (m[0] % 2) + i))
    return pl.pallas_call(
        with_meta(state_kernel),
        grid_spec=pltpu.PrefetchScalarGridSpec(
            num_scalar_prefetch=2,
            grid=(steps,),
            in_specs=[spec] * 2,
            out_specs=pl.BlockSpec((block, HD), lambda i, m, n: (i, 0)),
        ),
        out_shape=jax.ShapeDtypeStruct((cols // 2, HD), BF),
        compiler_params=params(62 * 1024 * 1024),
        name="state",
    )(*meta, k_lin, v_lin)


def inside_kernel(meta, q_ref, k_ref, v_ref, out_ref, mask_ref):
    rows = q_ref.shape[0]
    half = rows // 2
    first = meta[0] * rows

    @pl.when(pl.program_id(0) == 0)
    def _():
        start, _ = doc_rows(meta)
        pos = first + lax.broadcasted_iota(jnp.int32, (rows, HD), 0)
        began = jnp.max(jnp.where(pos >= start, start, -1), axis=1, keepdims=True) - first
        row = lax.broadcasted_iota(jnp.int32, (rows, rows), 0)
        col = lax.broadcasted_iota(jnp.int32, (rows, rows), 1)
        mask_ref[...] = jnp.where((col <= row) & (col >= began), 1.0, 0.0).astype(BF)

    for j in range(q_ref.shape[1] // HD):
        cols = slice(j * HD, (j + 1) * HD)
        pair = slice((j - j % 2) * HD, (j - j % 2 + 2) * HD)
        part = slice((j % 2) * HD, (j % 2 + 1) * HD)
        for i in range(2):
            at, upto = slice(i * half, (i + 1) * half), slice(0, (i + 1) * half)
            w = qk(q_ref[at, cols], k_ref[upto, cols]).astype(BF) * mask_ref[at, upto]
            o = jnp.dot(w, v_ref[upto, pair], preferred_element_type=F32)
            out_ref[at, cols] = o[:, part].astype(BF)


def inside_part(meta, q_lin, k_lin, v_lin, other, steps=2):
    rows, cols = q_lin.shape
    block = cols // (2 * steps)
    spec = pl.BlockSpec((rows, block), lambda i, m, n: (0, steps * ((m[0] + other) % 2) + i))
    return pl.pallas_call(
        with_meta(inside_kernel),
        grid_spec=pltpu.PrefetchScalarGridSpec(
            num_scalar_prefetch=2,
            grid=(steps,),
            in_specs=[spec] * 3,
            out_specs=pl.BlockSpec((rows, block), lambda i, m, n: (0, i)),
            scratch_shapes=[pltpu.VMEM((rows, rows), BF)],
        ),
        out_shape=jax.ShapeDtypeStruct((rows, cols // 2), BF),
        compiler_params=params(INSIDE_LIMIT),
        name="inside",
    )(*meta, q_lin, k_lin, v_lin)


def chip_kernel(rows, meta, own_ref, got_ref, out_ref):
    b = meta[0]
    second = b - b % 2 + 1
    whole = (doc_start(meta, second * rows + rows - 1) < second * rows).astype(F32)
    odd = (b % 2).astype(F32)
    scale_own = odd + (1.0 - odd) * whole
    scale_got = (1.0 - odd) + odd * whole
    out_ref[...] = (scale_own * own_ref[...].astype(F32) + scale_got * got_ref[...].astype(F32)).astype(BF)


def chip_state(meta, own, got, rows):
    return pl.pallas_call(
        with_meta(chip_kernel, rows),
        in_specs=[pl.BlockSpec(memory_space=pltpu.SMEM)] * 2 + [pl.BlockSpec(memory_space=pltpu.VMEM)] * 2,
        out_specs=pl.BlockSpec(memory_space=pltpu.VMEM),
        out_shape=jax.ShapeDtypeStruct(own.shape, BF),
        compiler_params=params(),
        name="chip_state",
    )(*meta, own, got)


def enter_kernel(rows, meta, one_ref, two_ref, own_ref, got_ref, mine_ref, pay_ref):
    b = meta[0]
    first = b - b % 2
    before = first * rows - 2 * rows
    chained = (doc_start(meta, first * rows - 1) < before).astype(F32)
    passes = (doc_start(meta, first * rows + rows - 1) < first * rows).astype(F32)
    odd = (b % 2).astype(F32)
    even = 1.0 - odd
    state = one_ref[...].astype(F32) + chained * two_ref[...].astype(F32)
    mine_ref[...] = ((even + odd * passes) * state + odd * got_ref[...].astype(F32)).astype(BF)
    pay_ref[...] = ((odd + even * passes) * state + even * own_ref[...].astype(F32)).astype(BF)


def entering(meta, one, two, own, got, rows):
    return pl.pallas_call(
        with_meta(enter_kernel, rows),
        in_specs=[pl.BlockSpec(memory_space=pltpu.SMEM)] * 2 + [pl.BlockSpec(memory_space=pltpu.VMEM)] * 4,
        out_specs=[pl.BlockSpec(memory_space=pltpu.VMEM)] * 2,
        out_shape=[jax.ShapeDtypeStruct(own.shape, BF)] * 2,
        compiler_params=params(),
        name="entering",
    )(*meta, one, two, own, got)


def carried_kernel(meta, q_ref, in_mine, in_other, mine_ref, other_ref, mix_ref, sum_ref, acc_ref):
    i = pl.program_id(0)
    rows = q_ref.shape[0]
    b = meta[0]
    first = b * rows
    reach = jnp.where(doc_start(meta, first) < first, doc_end(meta, first) - first, 0)
    row = lax.broadcasted_iota(jnp.int32, (rows, 2 * HD), 0)
    live = row < reach
    none = jnp.zeros((HD, HD), BF)

    def work(in_ref, state_ref, squares):
        for j in range(0, q_ref.shape[1] // HD, 2):
            cols = slice(j * HD, (j + 2) * HD)
            one, two = (state_ref[(j + e) * HD : (j + e + 1) * HD, :] for e in range(2))
            state = jnp.concatenate(
                [jnp.concatenate([one, none], axis=1), jnp.concatenate([none, two], axis=1)], axis=0
            )
            term = jnp.dot(q_ref[:, cols], state, preferred_element_type=F32)
            mix = in_ref[:, cols].astype(F32) + jnp.where(live, term, 0.0)
            square = mix * mix
            squares = squares + (square[:, :HD] + square[:, HD:])
            mix_ref[:, cols] = mix.astype(BF)
        return squares

    @pl.when(i == 0)
    def _():
        acc_ref[...] = work(in_mine, mine_ref, jnp.zeros((rows, HD), F32))

    @pl.when(i == 1)
    def _():
        squares = work(in_other, other_ref, acc_ref[...])
        sum_ref[...] = jnp.sum(squares.T, axis=0, keepdims=True)


def carried_part(meta, q_lin, in_mine, in_other, mine, other):
    rows, cols = q_lin.shape
    spec = pl.BlockSpec((rows, cols // 2), lambda i, m, n: (0, (i + m[0]) % 2))
    part = pl.BlockSpec((rows, cols // 2), lambda i, m, n: (0, 0))
    whole = pl.BlockSpec(mine.shape, lambda i, m, n: (0, 0))
    return pl.pallas_call(
        with_meta(carried_kernel),
        grid_spec=pltpu.PrefetchScalarGridSpec(
            num_scalar_prefetch=2,
            grid=(2,),
            in_specs=[spec, part, part, whole, whole],
            out_specs=[spec, pl.BlockSpec((1, rows), lambda i, m, n: (0, 0))],
            scratch_shapes=[pltpu.VMEM((rows, HD), F32)],
        ),
        out_shape=[jax.ShapeDtypeStruct((rows, cols), BF), jax.ShapeDtypeStruct((1, rows), F32)],
        compiler_params=params(),
        name="carried",
    )(*meta, q_lin, in_mine, in_other, mine, other)


def norm_kernel(mix_ref, *rest):
    *sum_refs, gain_ref, out_ref = rest
    rows = mix_ref.shape[0]
    total = sum(ref[...] for ref in sum_refs)
    inv = lax.rsqrt(total / (H * HD) + EPS)
    inv = jnp.broadcast_to(inv, (HD, rows)).T
    for j in range(mix_ref.shape[1] // HD):
        cols = slice(j * HD, (j + 1) * HD)
        out_ref[:, cols] = (mix_ref[:, cols].astype(F32) * inv * gain_ref[:, cols]).astype(BF)


def norm_part(mix, sums, gain, steps=2):
    rows, cols = mix.shape
    spec = pl.BlockSpec((rows, cols // steps), lambda i: (0, i))
    one = pl.BlockSpec((1, rows), lambda i: (0, 0))
    return pl.pallas_call(
        norm_kernel,
        grid=(steps,),
        in_specs=[spec] + [one] * len(sums) + [pl.BlockSpec((1, cols // steps), lambda i: (0, i))],
        out_specs=spec,
        out_shape=jax.ShapeDtypeStruct((rows, cols), BF),
        compiler_params=params(),
        name="norm",
    )(mix, *sums, gain)


def fill(docs, k_buf, v_buf, slot, k_ref, v_ref, first, count):
    at = pl.ds(pl.multiple_of(slot * count, count), count)
    k_buf[at, :HD] = k_ref[...]
    k_buf[at, HD:] = jnp.where(member(docs, first, count), 0.0, -BIG).astype(BF)
    v_buf[at, :HD] = v_ref[...]
    v_buf[at, HD:] = jnp.ones((count, HD), BF)


def mask_queries(docs, qx_ref, first, count):
    qx_ref[...] = jnp.where(member(docs, first, count), 1.0, 0.0).astype(BF)


def join_kernel(k_ref, v_ref, out_ref):
    width = k_ref.shape[1]
    out_ref[:, :width] = k_ref[...]
    out_ref[:, width:] = v_ref[...]


def joined(k, v):
    rows, width = k.shape
    return pl.pallas_call(
        join_kernel,
        in_specs=[pl.BlockSpec(memory_space=pltpu.VMEM)] * 2,
        out_specs=pl.BlockSpec(memory_space=pltpu.VMEM),
        out_shape=jax.ShapeDtypeStruct((rows, 2 * width), k.dtype),
        compiler_params=params(62 * 1024 * 1024),
        name="join",
    )(k, v)


def attend(q_ref, qx_ref, k_buf, v_buf, acc_ref, total_ref, keys, last):
    half = q_ref.shape[0]
    lane = lax.broadcasted_iota(jnp.int32, total_ref.shape, 1)
    packed = jnp.zeros(total_ref.shape, F32) if last else total_ref[...]
    if last:
        row = lax.broadcasted_iota(jnp.int32, (half, half), 0)
        col = lax.broadcasted_iota(jnp.int32, (half, half), 1)
        causal = col <= row

    def some(step, packed):
        for e in range(AT_ONCE):
            h = step * AT_ONCE + e
            cols = pl.ds(pl.multiple_of(h * HD, HD), HD)
            q = jnp.concatenate([q_ref[:, cols], qx_ref[...]], axis=1)
            p = jnp.exp2(qk(q, k_buf[keys, :]) * C2)
            if last:
                own = jnp.where(causal, p[:, -half:], 0.0)
                p = own if p.shape[1] == half else jnp.concatenate([p[:, :-half], own], axis=1)
            o = jnp.dot(p.astype(BF), v_buf[keys, :], preferred_element_type=F32)
            if last:
                acc_ref[:, cols] = o[:, :HD]
            else:
                acc_ref[:, cols] += o[:, :HD]
            packed = packed + jnp.where(lane == h, o[:, HD:], 0.0)
        return packed

    total_ref[...] = lax.fori_loop(0, q_ref.shape[1] // (HD * AT_ONCE), some, packed)


def each_length(start, end, most, unit, work):
    for count in range(1, most + 1):

        @pl.when(end - start == count)
        def _(count=count):
            work(pl.ds(pl.multiple_of(start * unit, unit), count * unit))


def near_kernel(meta, q_ref, k0, v0, k1, v1, k2, v2, k3, v3, *rest):
    acc_ref, total_ref, qx_ref, k_buf, v_buf = rest[-5:]
    rows = k0.shape[0]
    half = rows // 2
    i = pl.program_id(1)
    b = meta[0]
    odd = b % 2
    docs = doc_rows(meta)
    mask_queries(docs, qx_ref, b * rows + i * half, half)
    oldest = (b - 3) * rows

    @pl.when(i == 0)
    def _():
        spots = [(k0, v0, 3), (k2, v2, 1), (k3, v3, 2 - 2 * odd)]
        for k, v, slot in spots:
            fill(docs, k_buf, v_buf, slot, k, v, oldest + slot * rows, rows)

        @pl.when(odd == 1)
        def _():
            fill(docs, k_buf, v_buf, 2, k1, v1, oldest + 2 * rows, rows)

    began = doc_start(meta, b * rows + i * half) - oldest
    start = jnp.maximum(began, 2 * half * (1 - odd)) // half
    each_length(
        start,
        7 + i,
        8,
        half,
        lambda keys: attend(q_ref, qx_ref, k_buf, v_buf, acc_ref, total_ref, keys, True),
    )


def kv_specs(rows, groups, count):
    pair = [
        pl.BlockSpec((rows, HD), lambda g, i, m, n: (0, g)),
        pl.BlockSpec((rows, HD), lambda g, i, m, n: (0, groups + g)),
    ]
    return pair * count


def near_part(meta, q_soft, kvs):
    rows, cols = q_soft.shape
    groups = kvs[0].shape[1] // (2 * HD)
    width, half, n = cols // groups, rows // 2, len(kvs)
    return pl.pallas_call(
        with_meta(near_kernel),
        grid_spec=pltpu.PrefetchScalarGridSpec(
            num_scalar_prefetch=2,
            grid=(groups, 2),
            in_specs=[pl.BlockSpec((half, width), lambda g, i, m, n: (i, g))]
            + kv_specs(rows, groups, n),
            out_specs=[
                pl.BlockSpec((half, width), lambda g, i, m, n: (i, g)),
                pl.BlockSpec((half, HD), lambda g, i, m, n: (i, g)),
            ],
            scratch_shapes=[
                pltpu.VMEM((half, HD), BF),
                pltpu.VMEM((n * rows, 2 * HD), BF),
                pltpu.VMEM((n * rows, 2 * HD), BF),
            ],
        ),
        out_shape=[
            jax.ShapeDtypeStruct((rows, cols), F32),
            jax.ShapeDtypeStruct((rows, groups * HD), F32),
        ],
        compiler_params=params(),
        name="attend_near",
    )(*meta, q_soft, *[x for kv in kvs for x in (kv, kv)])


def far_kernel(meta, q_ref, acc_in, total_in, k0, v0, k1, v1, e0, e1, e2, e3, *rest):
    out_ref, acc_ref, total_ref, qx_ref, k_buf, v_buf, sem = rest
    rows = k0.shape[0]
    half = rows // 2
    heads = q_ref.shape[1] // HD
    groups = e0.shape[1] // (2 * HD)
    g = pl.program_id(0)
    i = pl.program_id(1)
    b = meta[0]
    twin = b + 1 - 2 * (b % 2)
    begins = [(b - 4) * rows, (twin - 4) * rows]
    docs = doc_rows(meta)
    mask_queries(docs, qx_ref, b * rows + i * half, half)
    acc_ref[...] = acc_in[...]
    total_ref[...] = total_in[...]
    began = doc_start(meta, b * rows + i * half) - begins[0]
    start = jnp.maximum(began, 0) // half
    end = 4 - 2 * (b % 2)

    @pl.when((i == 0) & (start < end))
    def _():
        for slot, (k, v) in enumerate(((k0, v0), (k1, v1))):
            fill(docs, k_buf, v_buf, slot, k, v, begins[slot], rows)

    each_length(
        start,
        end,
        4,
        half,
        lambda keys: attend(q_ref, qx_ref, k_buf, v_buf, acc_ref, total_ref, keys, False),
    )
    lane = lax.broadcasted_iota(jnp.int32, (half, HD), 1)
    total = total_ref[...]
    fine = ((total > LOW) & (total < HIGH)) | (lane >= heads)
    bad = jnp.max(jnp.where(fine, 0.0, 1.0)) > 0.0
    inverse = 1.0 / total
    for h in range(heads):
        cols = slice(h * HD, (h + 1) * HD)
        out_ref[:, cols] = (acc_ref[:, cols] * inverse[:, h : h + 1]).astype(BF)

    @pl.when(bad)
    def _():
        firsts = [b * rows, twin * rows, (b - 2) * rows, (twin - 2) * rows]
        for slot, (k, v) in enumerate(((k0, v0), (k1, v1))):
            fill(docs, k_buf, v_buf, slot, k, v, begins[slot], rows)
        for slot, (ref, first) in enumerate(zip((e0, e1, e2, e3), firsts)):
            at = slice((slot + 2) * rows, (slot + 3) * rows)
            for buf, off in ((k_buf, g), (v_buf, groups + g)):
                col = pl.multiple_of(off * HD, HD)
                copy = pltpu.make_async_copy(ref.at[:, pl.ds(col, HD)], buf.at[at, :HD], sem)
                copy.start()
                copy.wait()
            k_buf[at, HD:] = jnp.where(member(docs, first, rows), 0.0, -BIG).astype(BF)
        spots = [(s + 2, f) for s, f in enumerate(firsts)] + list(enumerate(begins))

        def redo(h, carry):
            cols = pl.ds(pl.multiple_of(h * HD, HD), HD)
            q = jnp.concatenate([q_ref[:, cols], qx_ref[...]], axis=1)
            top = jnp.full((half, 1), -BIG, F32)
            den = jnp.zeros((half, 1), F32)
            num = jnp.zeros((half, HD), F32)
            row = lax.broadcasted_iota(jnp.int32, (half, rows), 0) + (b * rows + i * half)
            col = lax.broadcasted_iota(jnp.int32, (half, rows), 1)
            for slot, first in spots:
                keys = slice(slot * rows, (slot + 1) * rows)
                s = jnp.where(col + first <= row, qk(q, k_buf[keys, :]) * C2, -BIG)
                new = jnp.maximum(top, jnp.max(s, axis=1, keepdims=True))
                p = jnp.exp2(s - new)
                fade = jnp.exp2(top - new)
                den = den * fade + jnp.sum(p, axis=1, keepdims=True)
                num = num * fade + jnp.dot(
                    p.astype(BF), v_buf[keys, :HD], preferred_element_type=F32
                )
                top = new
            out_ref[:, cols] = (num / den).astype(BF)
            return carry

        lax.fori_loop(0, heads, redo, 0)


def far_part(meta, q_soft, acc, total, kvs, spare):
    rows, cols = q_soft.shape
    groups = kvs[0].shape[1] // (2 * HD)
    width, half, n = cols // groups, rows // 2, len(kvs)
    slots = n + len(spare)
    operands = [*meta, q_soft, acc, total, *[x for kv in kvs for x in (kv, kv)], *spare]
    return pl.pallas_call(
        with_meta(far_kernel),
        grid_spec=pltpu.PrefetchScalarGridSpec(
            num_scalar_prefetch=2,
            grid=(groups, 2),
            in_specs=[
                pl.BlockSpec((half, width), lambda g, i, m, n: (i, g)),
                pl.BlockSpec((half, width), lambda g, i, m, n: (i, g)),
                pl.BlockSpec((half, HD), lambda g, i, m, n: (i, g)),
            ]
            + kv_specs(rows, groups, n)
            + [pl.BlockSpec(memory_space=pl.ANY)] * len(spare),
            out_specs=pl.BlockSpec((half, width), lambda g, i, m, n: (i, g)),
            scratch_shapes=[
                pltpu.VMEM((half, width), F32),
                pltpu.VMEM((half, HD), F32),
                pltpu.VMEM((half, HD), BF),
                pltpu.VMEM((slots * rows, 2 * HD), BF),
                pltpu.VMEM((slots * rows, 2 * HD), BF),
                pltpu.SemaphoreType.DMA,
            ],
        ),
        out_shape=jax.ShapeDtypeStruct((rows, cols), BF),
        compiler_params=params(),
        name="attend_far",
    )(*operands)


def after(value, *others):
    return lax.optimization_barrier((value, *others))[0]


def shards(q_lin, k_lin, v_lin, lin_gain, q_soft, k_soft, v_soft, doc_lengths):
    rows = q_lin.shape[0]
    peers = lax.axis_size("ctx")
    rings = lax.axis_size("head")
    next_chip = [(i, (i + 2) % peers) for i in range(peers)]
    twins = [(i, i ^ 1) for i in range(peers)]

    def forward(x):
        return lax.ppermute(x, "ctx", next_chip)

    def swap(x):
        return lax.ppermute(x, "ctx", twins)

    def shift(x, by):
        return lax.ppermute(x, "head", [(i, (i + by) % rings) for i in range(rings)])

    meta = (lax.axis_index("ctx").astype(jnp.int32).reshape(1), doc_lengths)
    kv = joined(k_soft, v_soft)
    kv_one = forward(kv)
    kv_twin = swap(kv)

    send, in_other = local_part(after(meta, kv), q_lin, k_lin, v_lin, 1)
    got = swap(send)
    keep = state_part(after(meta, send), k_lin, v_lin)
    chip = chip_state(after(meta, keep), keep, got, rows)
    one = forward(chip)
    in_mine = inside_part(after(meta, chip), q_lin, k_lin, v_lin, 0)

    kv_one = after(kv_one, chip)
    kv_one_twin = swap(kv_one)
    two = forward(after(one, in_mine))
    kv_two = forward(after(kv_one, one, in_mine))
    near_kvs = (kv, kv_twin, kv_one, kv_one_twin)
    acc, total = near_part(after(meta, in_mine, one), q_soft, near_kvs)

    mine, pay = entering(meta, one, after(two, acc), keep, got, rows)
    other = swap(pay)
    kv_two_twin = swap(after(kv_two, acc))
    mix, sums = carried_part(meta, q_lin, in_mine, in_other, mine, other)
    all_sums = [sums] + [shift(sums, d) for d in range(1, rings)]
    attn = far_part(after(meta, sums), q_soft, acc, total, (kv_two, kv_two_twin), near_kvs)
    all_sums = [after(x, attn) for x in all_sums]
    lin_out = norm_part(mix, all_sums, lin_gain.reshape(1, -1))
    return lin_out, attn


def solution(mesh):
    return jax.shard_map(
        shards,
        mesh=mesh,
        in_specs=(
            P("ctx", "head"),
            P("ctx", "head"),
            P("ctx", "head"),
            P("head"),
            P("ctx", "head"),
            P("ctx", "head"),
            P("ctx", "head"),
            P(),
        ),
        out_specs=(P("ctx", "head"), P("ctx", "head")),
        check_vma=False,
    )
```

```python
import math

import jax
import jax.numpy as jnp
from jax import lax
from jax.experimental import pallas as pl
from jax.experimental.pallas import tpu as pltpu
from jax.sharding import PartitionSpec as P

H = 64
HD = 128
EPS = 1e-05
BIG = 1e30
AT_ONCE = 4
LOW = 2.0**-60
HIGH = 2.0**100
C2 = math.log2(math.e) / math.sqrt(HD)
BF = jnp.bfloat16
F32 = jnp.float32
VMEM_LIMIT = 32 * 1024 * 1024
INSIDE_LIMIT = 60 * 1024 * 1024


class Meta:
    def __init__(self, place, lengths):
        self.place, self.lengths = place, lengths
        self.shape = (1 + lengths.shape[0],)

    def __getitem__(self, i):
        return self.place[0] if i == 0 else self.lengths[i - 1]


def with_meta(kernel, *leading):
    def wrapped(place, lengths, *refs):
        kernel(*leading, Meta(place, lengths), *refs)

    return wrapped


def doc_start(meta, pos):
    total, start = jnp.int32(0), jnp.int32(0)
    for d in range(1, meta.shape[0]):
        start = jnp.where(total <= pos, total, start)
        total = total + meta[d]
    return start


def doc_end(meta, pos):
    total, end = jnp.int32(0), jnp.int32(0)
    for d in range(1, meta.shape[0]):
        end = jnp.where(total <= pos, total + meta[d], end)
        total = total + meta[d]
    return end


def doc_rows(meta):
    lane = lax.broadcasted_iota(jnp.int32, (1, HD), 1)
    start = jnp.full((1, HD), 1 << 30, jnp.int32)
    end = jnp.full((1, HD), 1 << 30, jnp.int32)
    total = jnp.int32(0)
    for d in range(1, meta.shape[0]):
        start = jnp.where(lane == d - 1, total, start)
        total = total + meta[d]
        end = jnp.where(lane == d - 1, total, end)
    return start, end


def member(docs, first, count):
    start, end = docs
    pos = first + lax.broadcasted_iota(jnp.int32, (count, HD), 0)
    return (pos >= start) & (pos < end)


def params(limit=VMEM_LIMIT):
    return pltpu.CompilerParams(vmem_limit_bytes=limit)


def qk(q, k):
    return lax.dot_general(q, k, (((1,), (1,)), ((), ())), preferred_element_type=F32)


def local_kernel(meta, q_ref, k_ref, v_ref, state_ref, out_ref, mask_ref):
    rows = q_ref.shape[0]
    half = rows // 2
    first = meta[0] * rows
    tail = doc_start(meta, first + rows - 1) - first
    live = lax.broadcasted_iota(jnp.int32, (rows, 2 * HD), 0) >= tail

    @pl.when(pl.program_id(0) == 0)
    def _():
        start, _ = doc_rows(meta)
        pos = first + lax.broadcasted_iota(jnp.int32, (rows, HD), 0)
        began = jnp.max(jnp.where(pos >= start, start, -1), axis=1, keepdims=True) - first
        row = lax.broadcasted_iota(jnp.int32, (rows, rows), 0)
        col = lax.broadcasted_iota(jnp.int32, (rows, rows), 1)
        mask_ref[...] = jnp.where((col <= row) & (col >= began), 1.0, 0.0).astype(BF)

    for j in range(0, q_ref.shape[1] // HD, 2):
        pair = slice(j * HD, (j + 2) * HD)
        k = jnp.where(live, k_ref[:, pair], jnp.zeros((rows, 2 * HD), BF))
        s = lax.dot_general(
            k, v_ref[:, pair], (((0,), (0,)), ((), ())), preferred_element_type=F32
        ).astype(BF)
        for e in range(2):
            part = slice(e * HD, (e + 1) * HD)
            cols = slice((j + e) * HD, (j + e + 1) * HD)
            state_ref[cols, :] = s[part, part]
            for i in range(2):
                at, upto = slice(i * half, (i + 1) * half), slice(0, (i + 1) * half)
                w = qk(q_ref[at, cols], k_ref[upto, cols]).astype(BF) * mask_ref[at, upto]
                o = jnp.dot(w, v_ref[upto, pair], preferred_element_type=F32)
                out_ref[at, cols] = o[:, part].astype(BF)


def local_part(meta, q_lin, k_lin, v_lin, other, steps=2):
    rows, cols = q_lin.shape
    block = cols // (2 * steps)
    spec = pl.BlockSpec((rows, block), lambda i, m, n: (0, steps * ((m[0] + other) % 2) + i))
    return pl.pallas_call(
        with_meta(local_kernel),
        grid_spec=pltpu.PrefetchScalarGridSpec(
            num_scalar_prefetch=2,
            grid=(steps,),
            in_specs=[spec] * 3,
            out_specs=[
                pl.BlockSpec((block, HD), lambda i, m, n: (i, 0)),
                pl.BlockSpec((rows, block), lambda i, m, n: (0, i)),
            ],
            scratch_shapes=[pltpu.VMEM((rows, rows), BF)],
        ),
        out_shape=[
            jax.ShapeDtypeStruct((cols // 2, HD), BF),
            jax.ShapeDtypeStruct((rows, cols // 2), BF),
        ],
        compiler_params=params(61 * 1024 * 1024),
        name="local",
    )(*meta, q_lin, k_lin, v_lin)


def state_kernel(meta, k_ref, v_ref, state_ref):
    rows = k_ref.shape[0]
    first = meta[0] * rows
    tail = doc_start(meta, first + rows - 1) - first
    live = lax.broadcasted_iota(jnp.int32, (rows, 2 * HD), 0) >= tail
    for j in range(0, k_ref.shape[1] // HD, 2):
        pair = slice(j * HD, (j + 2) * HD)
        k = jnp.where(live, k_ref[:, pair], jnp.zeros((rows, 2 * HD), BF))
        s = lax.dot_general(
            k, v_ref[:, pair], (((0,), (0,)), ((), ())), preferred_element_type=F32
        ).astype(BF)
        for e in range(2):
            part = slice(e * HD, (e + 1) * HD)
            state_ref[(j + e) * HD : (j + e + 1) * HD, :] = s[part, part]


def state_part(meta, k_lin, v_lin, steps=2):
    rows, cols = k_lin.shape
    block = cols // (2 * steps)
    spec = pl.BlockSpec((rows, block), lambda i, m, n: (0, steps * (m[0] % 2) + i))
    return pl.pallas_call(
        with_meta(state_kernel),
        grid_spec=pltpu.PrefetchScalarGridSpec(
            num_scalar_prefetch=2,
            grid=(steps,),
            in_specs=[spec] * 2,
            out_specs=pl.BlockSpec((block, HD), lambda i, m, n: (i, 0)),
        ),
        out_shape=jax.ShapeDtypeStruct((cols // 2, HD), BF),
        compiler_params=params(62 * 1024 * 1024),
        name="state",
    )(*meta, k_lin, v_lin)


def inside_kernel(meta, q_ref, k_ref, v_ref, out_ref, mask_ref):
    rows = q_ref.shape[0]
    half = rows // 2
    first = meta[0] * rows

    @pl.when(pl.program_id(0) == 0)
    def _():
        start, _ = doc_rows(meta)
        pos = first + lax.broadcasted_iota(jnp.int32, (rows, HD), 0)
        began = jnp.max(jnp.where(pos >= start, start, -1), axis=1, keepdims=True) - first
        row = lax.broadcasted_iota(jnp.int32, (rows, rows), 0)
        col = lax.broadcasted_iota(jnp.int32, (rows, rows), 1)
        mask_ref[...] = jnp.where((col <= row) & (col >= began), 1.0, 0.0).astype(BF)

    for j in range(q_ref.shape[1] // HD):
        cols = slice(j * HD, (j + 1) * HD)
        pair = slice((j - j % 2) * HD, (j - j % 2 + 2) * HD)
        part = slice((j % 2) * HD, (j % 2 + 1) * HD)
        for i in range(2):
            at, upto = slice(i * half, (i + 1) * half), slice(0, (i + 1) * half)
            w = qk(q_ref[at, cols], k_ref[upto, cols]).astype(BF) * mask_ref[at, upto]
            o = jnp.dot(w, v_ref[upto, pair], preferred_element_type=F32)
            out_ref[at, cols] = o[:, part].astype(BF)


def inside_part(meta, q_lin, k_lin, v_lin, other, steps=2):
    rows, cols = q_lin.shape
    block = cols // (2 * steps)
    spec = pl.BlockSpec((rows, block), lambda i, m, n: (0, steps * ((m[0] + other) % 2) + i))
    return pl.pallas_call(
        with_meta(inside_kernel),
        grid_spec=pltpu.PrefetchScalarGridSpec(
            num_scalar_prefetch=2,
            grid=(steps,),
            in_specs=[spec] * 3,
            out_specs=pl.BlockSpec((rows, block), lambda i, m, n: (0, i)),
            scratch_shapes=[pltpu.VMEM((rows, rows), BF)],
        ),
        out_shape=jax.ShapeDtypeStruct((rows, cols // 2), BF),
        compiler_params=params(INSIDE_LIMIT),
        name="inside",
    )(*meta, q_lin, k_lin, v_lin)


def chip_kernel(rows, meta, own_ref, got_ref, out_ref):
    b = meta[0]
    second = b - b % 2 + 1
    whole = (doc_start(meta, second * rows + rows - 1) < second * rows).astype(F32)
    odd = (b % 2).astype(F32)
    scale_own = odd + (1.0 - odd) * whole
    scale_got = (1.0 - odd) + odd * whole
    out_ref[...] = (scale_own * own_ref[...].astype(F32) + scale_got * got_ref[...].astype(F32)).astype(BF)


def chip_state(meta, own, got, rows):
    return pl.pallas_call(
        with_meta(chip_kernel, rows),
        in_specs=[pl.BlockSpec(memory_space=pltpu.SMEM)] * 2 + [pl.BlockSpec(memory_space=pltpu.VMEM)] * 2,
        out_specs=pl.BlockSpec(memory_space=pltpu.VMEM),
        out_shape=jax.ShapeDtypeStruct(own.shape, BF),
        compiler_params=params(),
        name="chip_state",
    )(*meta, own, got)


def enter_kernel(rows, meta, one_ref, two_ref, own_ref, got_ref, mine_ref, pay_ref):
    b = meta[0]
    first = b - b % 2
    before = first * rows - 2 * rows
    chained = (doc_start(meta, first * rows - 1) < before).astype(F32)
    passes = (doc_start(meta, first * rows + rows - 1) < first * rows).astype(F32)
    odd = (b % 2).astype(F32)
    even = 1.0 - odd
    state = one_ref[...].astype(F32) + chained * two_ref[...].astype(F32)
    mine_ref[...] = ((even + odd * passes) * state + odd * got_ref[...].astype(F32)).astype(BF)
    pay_ref[...] = ((odd + even * passes) * state + even * own_ref[...].astype(F32)).astype(BF)


def entering(meta, one, two, own, got, rows):
    return pl.pallas_call(
        with_meta(enter_kernel, rows),
        in_specs=[pl.BlockSpec(memory_space=pltpu.SMEM)] * 2 + [pl.BlockSpec(memory_space=pltpu.VMEM)] * 4,
        out_specs=[pl.BlockSpec(memory_space=pltpu.VMEM)] * 2,
        out_shape=[jax.ShapeDtypeStruct(own.shape, BF)] * 2,
        compiler_params=params(),
        name="entering",
    )(*meta, one, two, own, got)


def carried_kernel(meta, q_ref, in_mine, in_other, mine_ref, other_ref, mix_ref, sum_ref, acc_ref):
    i = pl.program_id(0)
    rows = q_ref.shape[0]
    b = meta[0]
    first = b * rows
    reach = jnp.where(doc_start(meta, first) < first, doc_end(meta, first) - first, 0)
    row = lax.broadcasted_iota(jnp.int32, (rows, 2 * HD), 0)
    live = row < reach
    none = jnp.zeros((HD, HD), BF)

    def work(in_ref, state_ref, squares):
        for j in range(0, q_ref.shape[1] // HD, 2):
            cols = slice(j * HD, (j + 2) * HD)
            one, two = (state_ref[(j + e) * HD : (j + e + 1) * HD, :] for e in range(2))
            state = jnp.concatenate(
                [jnp.concatenate([one, none], axis=1), jnp.concatenate([none, two], axis=1)], axis=0
            )
            term = jnp.dot(q_ref[:, cols], state, preferred_element_type=F32)
            mix = in_ref[:, cols].astype(F32) + jnp.where(live, term, 0.0)
            square = mix * mix
            squares = squares + (square[:, :HD] + square[:, HD:])
            mix_ref[:, cols] = mix.astype(BF)
        return squares

    @pl.when(i == 0)
    def _():
        acc_ref[...] = work(in_mine, mine_ref, jnp.zeros((rows, HD), F32))

    @pl.when(i == 1)
    def _():
        squares = work(in_other, other_ref, acc_ref[...])
        sum_ref[...] = jnp.sum(squares.T, axis=0, keepdims=True)


def carried_part(meta, q_lin, in_mine, in_other, mine, other):
    rows, cols = q_lin.shape
    spec = pl.BlockSpec((rows, cols // 2), lambda i, m, n: (0, (i + m[0]) % 2))
    part = pl.BlockSpec((rows, cols // 2), lambda i, m, n: (0, 0))
    whole = pl.BlockSpec(mine.shape, lambda i, m, n: (0, 0))
    return pl.pallas_call(
        with_meta(carried_kernel),
        grid_spec=pltpu.PrefetchScalarGridSpec(
            num_scalar_prefetch=2,
            grid=(2,),
            in_specs=[spec, part, part, whole, whole],
            out_specs=[spec, pl.BlockSpec((1, rows), lambda i, m, n: (0, 0))],
            scratch_shapes=[pltpu.VMEM((rows, HD), F32)],
        ),
        out_shape=[jax.ShapeDtypeStruct((rows, cols), BF), jax.ShapeDtypeStruct((1, rows), F32)],
        compiler_params=params(),
        name="carried",
    )(*meta, q_lin, in_mine, in_other, mine, other)


def norm_kernel(mix_ref, *rest):
    *sum_refs, gain_ref, out_ref = rest
    rows = mix_ref.shape[0]
    total = sum(ref[...] for ref in sum_refs)
    inv = lax.rsqrt(total / (H * HD) + EPS)
    inv = jnp.broadcast_to(inv, (HD, rows)).T
    for j in range(mix_ref.shape[1] // HD):
        cols = slice(j * HD, (j + 1) * HD)
        out_ref[:, cols] = (mix_ref[:, cols].astype(F32) * inv * gain_ref[:, cols]).astype(BF)


def norm_part(mix, sums, gain, steps=2):
    rows, cols = mix.shape
    spec = pl.BlockSpec((rows, cols // steps), lambda i: (0, i))
    one = pl.BlockSpec((1, rows), lambda i: (0, 0))
    return pl.pallas_call(
        norm_kernel,
        grid=(steps,),
        in_specs=[spec] + [one] * len(sums) + [pl.BlockSpec((1, cols // steps), lambda i: (0, i))],
        out_specs=spec,
        out_shape=jax.ShapeDtypeStruct((rows, cols), BF),
        compiler_params=params(),
        name="norm",
    )(mix, *sums, gain)


def fill(docs, k_buf, v_buf, slot, k_ref, v_ref, first, count):
    at = pl.ds(pl.multiple_of(slot * count, count), count)
    k_buf[at, :HD] = k_ref[...]
    k_buf[at, HD:] = jnp.where(member(docs, first, count), 0.0, -BIG).astype(BF)
    v_buf[at, :HD] = v_ref[...]
    v_buf[at, HD:] = jnp.ones((count, HD), BF)


def mask_queries(docs, qx_ref, first, count):
    qx_ref[...] = jnp.where(member(docs, first, count), 1.0, 0.0).astype(BF)


def join_kernel(k_ref, v_ref, out_ref):
    width = k_ref.shape[1]
    out_ref[:, :width] = k_ref[...]
    out_ref[:, width:] = v_ref[...]


def joined(k, v):
    rows, width = k.shape
    return pl.pallas_call(
        join_kernel,
        in_specs=[pl.BlockSpec(memory_space=pltpu.VMEM)] * 2,
        out_specs=pl.BlockSpec(memory_space=pltpu.VMEM),
        out_shape=jax.ShapeDtypeStruct((rows, 2 * width), k.dtype),
        compiler_params=params(62 * 1024 * 1024),
        name="join",
    )(k, v)


def attend(q_ref, qx_ref, k_buf, v_buf, acc_ref, total_ref, keys, last):
    half = q_ref.shape[0]
    lane = lax.broadcasted_iota(jnp.int32, total_ref.shape, 1)
    packed = jnp.zeros(total_ref.shape, F32) if last else total_ref[...]
    if last:
        row = lax.broadcasted_iota(jnp.int32, (half, half), 0)
        col = lax.broadcasted_iota(jnp.int32, (half, half), 1)
        causal = col <= row

    at_once = AT_ONCE if last else 2 * AT_ONCE

    def some(step, packed):
        for e in range(at_once):
            h = step * at_once + e
            cols = pl.ds(pl.multiple_of(h * HD, HD), HD)
            q = jnp.concatenate([q_ref[:, cols], qx_ref[...]], axis=1)
            p = jnp.exp2(qk(q, k_buf[keys, :]) * C2)
            if last:
                own = jnp.where(causal, p[:, -half:], 0.0)
                p = own if p.shape[1] == half else jnp.concatenate([p[:, :-half], own], axis=1)
            o = jnp.dot(p.astype(BF), v_buf[keys, :], preferred_element_type=F32)
            if last:
                acc_ref[:, cols] = o[:, :HD]
            else:
                acc_ref[:, cols] += o[:, :HD]
            packed = packed + jnp.where(lane == h, o[:, HD:], 0.0)
        return packed

    total_ref[...] = lax.fori_loop(0, q_ref.shape[1] // (HD * at_once), some, packed)


def each_length(start, end, most, unit, work):
    for count in range(1, most + 1):

        @pl.when(end - start == count)
        def _(count=count):
            work(pl.ds(pl.multiple_of(start * unit, unit), count * unit))


def near_kernel(meta, q_ref, k0, v0, k1, v1, k2, v2, k3, v3, *rest):
    acc_ref, total_ref, qx_ref, k_buf, v_buf = rest[-5:]
    rows = k0.shape[0]
    half = rows // 2
    i = pl.program_id(1)
    b = meta[0]
    odd = b % 2
    docs = doc_rows(meta)
    mask_queries(docs, qx_ref, b * rows + i * half, half)
    oldest = (b - 3) * rows

    @pl.when(i == 0)
    def _():
        spots = [(k0, v0, 3), (k2, v2, 1), (k3, v3, 2 - 2 * odd)]
        for k, v, slot in spots:
            fill(docs, k_buf, v_buf, slot, k, v, oldest + slot * rows, rows)

        @pl.when(odd == 1)
        def _():
            fill(docs, k_buf, v_buf, 2, k1, v1, oldest + 2 * rows, rows)

    began = doc_start(meta, b * rows + i * half) - oldest
    start = jnp.maximum(began, 2 * half * (1 - odd)) // half
    each_length(
        start,
        7 + i,
        8,
        half,
        lambda keys: attend(q_ref, qx_ref, k_buf, v_buf, acc_ref, total_ref, keys, True),
    )


def kv_specs(rows, groups, count):
    pair = [
        pl.BlockSpec((rows, HD), lambda g, i, m, n: (0, g)),
        pl.BlockSpec((rows, HD), lambda g, i, m, n: (0, groups + g)),
    ]
    return pair * count


def near_part(meta, q_soft, kvs):
    rows, cols = q_soft.shape
    groups = kvs[0].shape[1] // (2 * HD)
    width, half, n = cols // groups, rows // 2, len(kvs)
    return pl.pallas_call(
        with_meta(near_kernel),
        grid_spec=pltpu.PrefetchScalarGridSpec(
            num_scalar_prefetch=2,
            grid=(groups, 2),
            in_specs=[pl.BlockSpec((half, width), lambda g, i, m, n: (i, g))]
            + kv_specs(rows, groups, n),
            out_specs=[
                pl.BlockSpec((half, width), lambda g, i, m, n: (i, g)),
                pl.BlockSpec((half, HD), lambda g, i, m, n: (i, g)),
            ],
            scratch_shapes=[
                pltpu.VMEM((half, HD), BF),
                pltpu.VMEM((n * rows, 2 * HD), BF),
                pltpu.VMEM((n * rows, 2 * HD), BF),
            ],
        ),
        out_shape=[
            jax.ShapeDtypeStruct((rows, cols), F32),
            jax.ShapeDtypeStruct((rows, groups * HD), F32),
        ],
        compiler_params=params(),
        name="attend_near",
    )(*meta, q_soft, *[x for kv in kvs for x in (kv, kv)])


def far_kernel(meta, q_ref, acc_in, total_in, k0, v0, k1, v1, e0, e1, e2, e3, *rest):
    out_ref, acc_ref, total_ref, qx_ref, k_buf, v_buf, sem = rest
    rows = k0.shape[0]
    half = rows // 2
    heads = q_ref.shape[1] // HD
    groups = e0.shape[1] // (2 * HD)
    g = pl.program_id(0)
    i = pl.program_id(1)
    b = meta[0]
    twin = b + 1 - 2 * (b % 2)
    begins = [(b - 4) * rows, (twin - 4) * rows]
    docs = doc_rows(meta)
    mask_queries(docs, qx_ref, b * rows + i * half, half)
    acc_ref[...] = acc_in[...]
    total_ref[...] = total_in[...]
    began = doc_start(meta, b * rows + i * half) - begins[0]
    start = jnp.maximum(began, 0) // half
    end = 4 - 2 * (b % 2)

    @pl.when((i == 0) & (start < end))
    def _():
        for slot, (k, v) in enumerate(((k0, v0), (k1, v1))):
            fill(docs, k_buf, v_buf, slot, k, v, begins[slot], rows)

    each_length(
        start,
        end,
        4,
        half,
        lambda keys: attend(q_ref, qx_ref, k_buf, v_buf, acc_ref, total_ref, keys, False),
    )
    lane = lax.broadcasted_iota(jnp.int32, (half, HD), 1)
    total = total_ref[...]
    fine = ((total > LOW) & (total < HIGH)) | (lane >= heads)
    bad = jnp.max(jnp.where(fine, 0.0, 1.0)) > 0.0
    inverse = 1.0 / total
    for h in range(heads):
        cols = slice(h * HD, (h + 1) * HD)
        out_ref[:, cols] = (acc_ref[:, cols] * inverse[:, h : h + 1]).astype(BF)

    @pl.when(bad)
    def _():
        firsts = [b * rows, twin * rows, (b - 2) * rows, (twin - 2) * rows]
        for slot, (k, v) in enumerate(((k0, v0), (k1, v1))):
            fill(docs, k_buf, v_buf, slot, k, v, begins[slot], rows)
        for slot, (ref, first) in enumerate(zip((e0, e1, e2, e3), firsts)):
            at = slice((slot + 2) * rows, (slot + 3) * rows)
            for buf, off in ((k_buf, g), (v_buf, groups + g)):
                col = pl.multiple_of(off * HD, HD)
                copy = pltpu.make_async_copy(ref.at[:, pl.ds(col, HD)], buf.at[at, :HD], sem)
                copy.start()
                copy.wait()
            k_buf[at, HD:] = jnp.where(member(docs, first, rows), 0.0, -BIG).astype(BF)
        spots = [(s + 2, f) for s, f in enumerate(firsts)] + list(enumerate(begins))

        def redo(h, carry):
            cols = pl.ds(pl.multiple_of(h * HD, HD), HD)
            q = jnp.concatenate([q_ref[:, cols], qx_ref[...]], axis=1)
            top = jnp.full((half, 1), -BIG, F32)
            den = jnp.zeros((half, 1), F32)
            num = jnp.zeros((half, HD), F32)
            row = lax.broadcasted_iota(jnp.int32, (half, rows), 0) + (b * rows + i * half)
            col = lax.broadcasted_iota(jnp.int32, (half, rows), 1)
            for slot, first in spots:
                keys = slice(slot * rows, (slot + 1) * rows)
                s = jnp.where(col + first <= row, qk(q, k_buf[keys, :]) * C2, -BIG)
                new = jnp.maximum(top, jnp.max(s, axis=1, keepdims=True))
                p = jnp.exp2(s - new)
                fade = jnp.exp2(top - new)
                den = den * fade + jnp.sum(p, axis=1, keepdims=True)
                num = num * fade + jnp.dot(
                    p.astype(BF), v_buf[keys, :HD], preferred_element_type=F32
                )
                top = new
            out_ref[:, cols] = (num / den).astype(BF)
            return carry

        lax.fori_loop(0, heads, redo, 0)


def far_part(meta, q_soft, acc, total, kvs, spare):
    rows, cols = q_soft.shape
    groups = kvs[0].shape[1] // (2 * HD)
    width, half, n = cols // groups, rows // 2, len(kvs)
    slots = n + len(spare)
    operands = [*meta, q_soft, acc, total, *[x for kv in kvs for x in (kv, kv)], *spare]
    return pl.pallas_call(
        with_meta(far_kernel),
        grid_spec=pltpu.PrefetchScalarGridSpec(
            num_scalar_prefetch=2,
            grid=(groups, 2),
            in_specs=[
                pl.BlockSpec((half, width), lambda g, i, m, n: (i, g)),
                pl.BlockSpec((half, width), lambda g, i, m, n: (i, g)),
                pl.BlockSpec((half, HD), lambda g, i, m, n: (i, g)),
            ]
            + kv_specs(rows, groups, n)
            + [pl.BlockSpec(memory_space=pl.ANY)] * len(spare),
            out_specs=pl.BlockSpec((half, width), lambda g, i, m, n: (i, g)),
            scratch_shapes=[
                pltpu.VMEM((half, width), F32),
                pltpu.VMEM((half, HD), F32),
                pltpu.VMEM((half, HD), BF),
                pltpu.VMEM((slots * rows, 2 * HD), BF),
                pltpu.VMEM((slots * rows, 2 * HD), BF),
                pltpu.SemaphoreType.DMA,
            ],
        ),
        out_shape=jax.ShapeDtypeStruct((rows, cols), BF),
        compiler_params=params(),
        name="attend_far",
    )(*operands)


def after(value, *others):
    return lax.optimization_barrier((value, *others))[0]


def shards(q_lin, k_lin, v_lin, lin_gain, q_soft, k_soft, v_soft, doc_lengths):
    rows = q_lin.shape[0]
    peers = lax.axis_size("ctx")
    rings = lax.axis_size("head")
    next_chip = [(i, (i + 2) % peers) for i in range(peers)]
    twins = [(i, i ^ 1) for i in range(peers)]

    def forward(x):
        return lax.ppermute(x, "ctx", next_chip)

    def swap(x):
        return lax.ppermute(x, "ctx", twins)

    def shift(x, by):
        return lax.ppermute(x, "head", [(i, (i + by) % rings) for i in range(rings)])

    meta = (lax.axis_index("ctx").astype(jnp.int32).reshape(1), doc_lengths)
    kv = joined(k_soft, v_soft)
    kv_one = forward(kv)
    kv_twin = swap(kv)

    send, in_other = local_part(after(meta, kv), q_lin, k_lin, v_lin, 1)
    got = swap(send)
    keep = state_part(after(meta, send), k_lin, v_lin)
    chip = chip_state(after(meta, keep), keep, got, rows)
    one = forward(chip)
    in_mine = inside_part(after(meta, chip), q_lin, k_lin, v_lin, 0)

    kv_one = after(kv_one, chip)
    kv_one_twin = swap(kv_one)
    two = forward(after(one, in_mine))
    kv_two = forward(after(kv_one, one, in_mine))
    near_kvs = (kv, kv_twin, kv_one, kv_one_twin)
    acc, total = near_part(after(meta, in_mine, one), q_soft, near_kvs)

    mine, pay = entering(meta, one, after(two, acc), keep, got, rows)
    other = swap(pay)
    kv_two_twin = swap(after(kv_two, acc))
    mix, sums = carried_part(meta, q_lin, in_mine, in_other, mine, other)
    all_sums = [sums] + [shift(sums, d) for d in range(1, rings)]
    attn = far_part(after(meta, sums), q_soft, acc, total, (kv_two, kv_two_twin), near_kvs)
    all_sums = [after(x, attn) for x in all_sums]
    lin_out = norm_part(mix, all_sums, lin_gain.reshape(1, -1))
    return lin_out, attn


def solution(mesh):
    return jax.shard_map(
        shards,
        mesh=mesh,
        in_specs=(
            P("ctx", "head"),
            P("ctx", "head"),
            P("ctx", "head"),
            P("head"),
            P("ctx", "head"),
            P("ctx", "head"),
            P("ctx", "head"),
            P(),
        ),
        out_specs=(P("ctx", "head"), P("ctx", "head")),
        check_vma=False,
    )
```
